512 devices in a mesh: dp: 4 (over y), row: 8 (over x, core), col: 16 (over z).
Axes of the slice: x: 4, y: 4, z: 16, core: 2. Of those that a mesh axis runs over, the one named last changes fastest.
Arguments:
- tokens: bfloat16 [512, 8192], P(('dp', 'col'), 'row'), may hold values from -6 to 6
- grad_out: bfloat16 [512, 8192], P(('dp', 'col'), 'row'), may hold values from -6 to 6
- gate_blocks: bfloat16 [8, 16, 44, 4096], P('row', 'col'), may hold values from -0.21875 to 0.21875
- up_blocks: bfloat16 [8, 16, 44, 4096], P('row', 'col'), may hold values from -0.21875 to 0.21875
- down_blocks: bfloat16 [8, 16, 44, 4096], P('row', 'col'), may hold values from -0.109375 to 0.109375
- block_index: int32 [3, 8, 16, 2, 44], P(None, 'row', 'col'), may hold values from 0 to 27, as said below
- block_count: int32 [3, 8, 16], P(None, 'row', 'col'), may hold values from 11 to 44, as said below
Outputs:
- mixed: bfloat16 [512, 8192], P(('dp', 'col'), 'row')
- tokens_grad: bfloat16 [512, 8192], P(('dp', 'col'), 'row')
- gate_grad: bfloat16 [8, 16, 44, 4096], P('row', 'col')
- up_grad: bfloat16 [8, 16, 44, 4096], P('row', 'col')
- down_grad: bfloat16 [8, 16, 44, 4096], P('row', 'col')
The draws below stay inside these ranges and needn't reach their ends.
Inputs may be any that keep to these rules, and one draw needn't show every extreme that they name: block_index[m, r, c, 0, s] is a block row of the tile, below 16, and block_index[m, r, c, 1, s] a block column, below 28; the 44 slots of one list name distinct blocks. Slots s >= block_count[m, r, c] are not part of the matrix. Every draw has a list with exactly 44 live slots.
All inputs are finite; a program needn't handle non-finite values.
Results may differ from the reference program's by a relative error of at most 0.03.
Values may be sent and summed in bfloat16 or wider, within the bound.
No kernel may reach another device: no remote copies, remote signals or barrier semaphores. Data moves between devices by JAX's collectives and lax.ppermute only.
A program may use at most 64 MiB of HBM per device.

```python
import jax
import jax.numpy as jnp
from jax import lax

D = 8192
FF = 28672
BS = 64
TILE_BROWS = 16
TILE_BCOLS = 28
TILE_MAX = 44
ROW_TILES = 8
COL_TILES = 16
TOKENS = 512
N_DP = 4


def draw_block_index(key, part):
    key = jax.random.fold_in(key, 11)
    list_count = 3 * ROW_TILES * COL_TILES
    places = TILE_BROWS * TILE_BCOLS
    subkeys = jax.random.split(key, list_count)
    order_lists = jax.vmap(lambda single: jax.random.permutation(single, places))(subkeys)
    chosen = order_lists[:, :TILE_MAX]
    block_rows = chosen // TILE_BCOLS
    block_cols = chosen % TILE_BCOLS
    stacked = jnp.stack([block_rows, block_cols], axis=1)
    return stacked.reshape(3, ROW_TILES, COL_TILES, 2, TILE_MAX).astype(jnp.int32)


def draw_block_count(key, part):
    key = jax.random.fold_in(key, 23)
    list_total = 3 * ROW_TILES * COL_TILES
    lowest = max(TILE_MAX // 4, 1)
    counts = jax.random.randint(jax.random.fold_in(key, 1), (list_total,), lowest, 3 * TILE_MAX // 4 + 1)
    fullest = jax.random.randint(jax.random.fold_in(key, 2), (), 0, list_total)
    offset = jax.random.randint(jax.random.fold_in(key, 3), (), 1, list_total)
    counts = counts.at[fullest].set(TILE_MAX)
    counts = counts.at[(fullest + offset) % list_total].set(lowest)
    return counts.reshape(3, ROW_TILES, COL_TILES).astype(jnp.int32)


def steps_of(key, extent, cuts, low, high):
    loudness = 1.0
    for dim, blocks in cuts:
        draws = jax.random.uniform(jax.random.fold_in(jax.random.fold_in(key, 6), dim), (blocks,), jnp.float32, low / len(cuts), high / len(cuts))
        loudness = loudness * jnp.repeat(jnp.exp(draws), extent[dim] // blocks).reshape((-1,) + (1,) * (len(extent) - 1 - dim))
    return loudness


def normal_values(rng, extent, deviation, most, shards=(), held_as=jnp.bfloat16):
    entries = deviation * jax.random.normal(rng, extent, jnp.float32)
    if shards:
        entries = entries * steps_of(rng, extent, shards, -0.22, 0.18)
    return jnp.clip(entries, -most, most).astype(held_as)


def setup_inputs(seed: int = 0) -> dict:
    splits = jax.random.split(jax.random.key(seed), 8)
    tokens = normal_values(splits[0], (TOKENS, D), 1.0, 6.0, ((0, 64), (1, 8)))
    grad_out = normal_values(splits[1], (TOKENS, D), 1.0, 6.0, ((0, 64), (1, 8)))
    gate_blocks = normal_values(splits[2], (ROW_TILES, COL_TILES, TILE_MAX, BS * BS), (D // 10) ** -0.5, 0.21875, ((0, 8), (1, 16)))
    up_blocks = normal_values(splits[3], (ROW_TILES, COL_TILES, TILE_MAX, BS * BS), (D // 10) ** -0.5, 0.21875, ((0, 8), (1, 16)))
    down_blocks = normal_values(splits[4], (ROW_TILES, COL_TILES, TILE_MAX, BS * BS), (FF // 10) ** -0.5, 0.109375, ((0, 8), (1, 16)))
    block_index = draw_block_index(jax.random.fold_in(splits[7], 71), 0)
    block_count = draw_block_count(jax.random.fold_in(splits[7], 71), 0)
    return dict(tokens=tokens, grad_out=grad_out, gate_blocks=gate_blocks, up_blocks=up_blocks, down_blocks=down_blocks, block_index=block_index, block_count=block_count)


def slot_view(band_rows, pick_ids, block_width):
    shaped = band_rows.reshape(band_rows.shape[0] // block_width, block_width, band_rows.shape[1])
    return jnp.take(shaped, pick_ids, axis=0)


def collect(products, places, live_mask, count_out):
    masked = products * live_mask[:, None, None]
    summed = jnp.zeros((count_out, products.shape[1], products.shape[2]), jnp.float32).at[places].add(masked)
    return summed.reshape(count_out * products.shape[1], products.shape[2])


def spread(blocks, source, pick_ids, places, live_mask, count_out):
    slot_data = slot_view(source, pick_ids, blocks.shape[1]).astype(jnp.float32)
    products = jnp.einsum('sdf,sdt->sft', blocks.astype(jnp.float32), slot_data, precision=lax.Precision.HIGHEST)
    return collect(products, places, live_mask, count_out)


def fold_back(blocks, source, pick_ids, places, live_mask, count_out):
    slot_data = slot_view(source, pick_ids, blocks.shape[1]).astype(jnp.float32)
    products = jnp.einsum('sdf,sft->sdt', blocks.astype(jnp.float32), slot_data, precision=lax.Precision.HIGHEST)
    return collect(products, places, live_mask, count_out)


def there_and_back(values):
    return lax.optimization_barrier(values.astype(jnp.bfloat16)).astype(jnp.float32)


def reference(tokens, grad_out, gate_blocks, up_blocks, down_blocks, block_index, block_count):
    tok_cols = tokens.T
    grad_cols = grad_out.T
    total_tok = tokens.shape[0]
    band_height = D // ROW_TILES
    band_span_width = FF // COL_TILES
    weights = jnp.stack([gate_blocks, up_blocks, down_blocks]).reshape(3, ROW_TILES, COL_TILES, TILE_MAX, BS, BS)
    live_mask = (jnp.arange(TILE_MAX, dtype=jnp.int32)[None, None, None, :] < block_count[:, :, :, None]).astype(jnp.float32)

    def row_band(values, row_id):
        return lax.dynamic_slice_in_dim(values, row_id * band_height, band_height, 0)

    def col_band(values, col_id):
        return lax.dynamic_slice_in_dim(values, col_id * band_span_width, band_span_width, 0)

    def over_rows(source, first_id, second_id):
        def column_pass(col_id):
            def add_row(carry, row_id):
                band_source = row_band(source, row_id)
                first_term = spread(weights[first_id, row_id, col_id], band_source, block_index[first_id, row_id, col_id, 0], block_index[first_id, row_id, col_id, 1], live_mask[first_id, row_id, col_id], TILE_BCOLS)
                second_term = spread(weights[second_id, row_id, col_id], band_source, block_index[second_id, row_id, col_id, 0], block_index[second_id, row_id, col_id, 1], live_mask[second_id, row_id, col_id], TILE_BCOLS)
                return (carry[0] + there_and_back(first_term), carry[1] + there_and_back(second_term)), None

            start = jnp.zeros((band_span_width, total_tok), jnp.float32)
            band_sums, unused = lax.scan(add_row, (start, start), jnp.arange(ROW_TILES, dtype=jnp.int32))
            return band_sums

        first_bands, second_bands = lax.map(column_pass, jnp.arange(COL_TILES, dtype=jnp.int32))
        return first_bands.reshape(FF, total_tok), second_bands.reshape(FF, total_tok)

    gate_full, up_full = over_rows(tok_cols, 0, 1)
    hidden = (jax.nn.silu(gate_full) * up_full).astype(jnp.bfloat16)

    def down_row(row_id):
        def add_col(carry, col_id):
            down_term = fold_back(weights[2, row_id, col_id], col_band(hidden, col_id), block_index[2, row_id, col_id, 1], block_index[2, row_id, col_id, 0], live_mask[2, row_id, col_id], TILE_BROWS)
            return carry + there_and_back(down_term), None

        start = jnp.zeros((band_height, total_tok), jnp.float32)
        band_total_sum, unused = lax.scan(add_col, start, jnp.arange(COL_TILES, dtype=jnp.int32))
        return band_total_sum

    out_bands = lax.map(down_row, jnp.arange(ROW_TILES, dtype=jnp.int32))
    mixed = out_bands.reshape(D, total_tok).T.astype(jnp.bfloat16)

    hgrad_full, unused_copy = over_rows(grad_cols, 2, 2)
    gate_sigmoid = jax.nn.sigmoid(gate_full)
    up_grad_h = (hgrad_full * gate_full * gate_sigmoid).astype(jnp.bfloat16)
    gate_grad_h = (hgrad_full * up_full * gate_sigmoid * (1.0 + gate_full * (1.0 - gate_sigmoid))).astype(jnp.bfloat16)

    def input_row(row_id):
        def add_col(carry, col_id):
            gate_term = fold_back(weights[0, row_id, col_id], col_band(gate_grad_h, col_id), block_index[0, row_id, col_id, 1], block_index[0, row_id, col_id, 0], live_mask[0, row_id, col_id], TILE_BROWS)
            up_term = fold_back(weights[1, row_id, col_id], col_band(up_grad_h, col_id), block_index[1, row_id, col_id, 1], block_index[1, row_id, col_id, 0], live_mask[1, row_id, col_id], TILE_BROWS)
            return carry + there_and_back(gate_term + up_term), None

        start = jnp.zeros((band_height, total_tok), jnp.float32)
        band_total_sum, unused = lax.scan(add_col, start, jnp.arange(COL_TILES, dtype=jnp.int32))
        return band_total_sum

    in_bands = lax.map(input_row, jnp.arange(ROW_TILES, dtype=jnp.int32))
    tokens_grad = in_bands.reshape(D, total_tok).T.astype(jnp.bfloat16)

    group_size = total_tok // N_DP

    def tile_grads(tile_id):
        row_id = tile_id // COL_TILES
        col_id = tile_id % COL_TILES
        triples = ((0, row_band(tok_cols, row_id), col_band(gate_grad_h, col_id)), (1, row_band(tok_cols, row_id), col_band(up_grad_h, col_id)), (2, row_band(grad_cols, row_id), col_band(hidden, col_id)))
        results = []
        for matrix_id, left_band, right_band in triples:
            left_slot_list = slot_view(left_band, block_index[matrix_id, row_id, col_id, 0], BS).astype(jnp.float32).reshape(TILE_MAX, BS, N_DP, group_size)
            right_slot_list = slot_view(right_band, block_index[matrix_id, row_id, col_id, 1], BS).astype(jnp.float32).reshape(TILE_MAX, BS, N_DP, group_size)
            group_member_count = jnp.einsum('vhab,vcab->avhc', left_slot_list, right_slot_list, precision=lax.Precision.HIGHEST)
            summed = jnp.sum(there_and_back(group_member_count), axis=0) * live_mask[matrix_id, row_id, col_id][:, None, None]
            results.append(summed.astype(jnp.bfloat16).reshape(TILE_MAX, BS * BS))
        return results[0], results[1], results[2]

    gate_grad, up_grad, down_grad = lax.map(tile_grads, jnp.arange(ROW_TILES * COL_TILES, dtype=jnp.int32))
    shape_out = (ROW_TILES, COL_TILES, TILE_MAX, BS * BS)
    return (mixed, tokens_grad, gate_grad.reshape(shape_out), up_grad.reshape(shape_out), down_grad.reshape(shape_out))
```

```python
import functools

import jax
import jax.numpy as jnp
from jax import lax
from jax.experimental import pallas as pl
from jax.experimental.pallas import tpu as pltpu
from jax.sharding import PartitionSpec as P

BS = 64
UNROLL = 4
VMEM = pl.BlockSpec(memory_space=pltpu.VMEM)
SMEM = pl.BlockSpec(memory_space=pltpu.SMEM)
PARAMS = pltpu.CompilerParams(vmem_limit_bytes=40 * 1024 * 1024)
F32 = jnp.float32
BF16 = jnp.bfloat16


def for_slots(count, step):
    def group(g, carry):
        for u in range(UNROLL):
            s = g * UNROLL + u
            step(s, s < count)
        return carry

    lax.fori_loop(0, (count + UNROLL - 1) // UNROLL, group, 0)


def rows_of(block):
    return pl.ds(pl.multiple_of(block * BS, BS), BS)


def spread_kernel(index, count, wide, gate, up, down, cols, parts, total):
    n_col, pair, width = wide.shape
    half = pair // 2
    toks = n_col * half
    for j in range(0, width, 128):
        piece = wide[:, :, j : j + 128].astype(F32).reshape(n_col, 2, half, 128)
        for side in range(2):
            cols[side, j : j + 128, :] = piece[:, side].reshape(toks, 128).T.astype(BF16)
    total[...] = jnp.zeros_like(total)
    for m, weights in enumerate((gate, up, down)):
        side = m // 2

        def step(s, live):
            block = jnp.where(live, weights[s], jnp.zeros_like(weights[s]))
            source = cols[side, rows_of(index[m, 0, s]), :]
            place = rows_of(index[m, 1, s])
            total[m, place, :] += lax.dot_general(
                block, source, (((0,), (0,)), ((), ())), preferred_element_type=F32
            )

        for_slots(count[m], step)
    share = parts.shape[2]
    for j in range(parts.shape[0]):
        for m in range(3):
            parts[j, m] = total[m, j * share : (j + 1) * share, :].astype(BF16)


def hidden_kernel(terms, out):
    sums = [terms[0, m].astype(F32) for m in range(3)]
    for j in range(1, terms.shape[0]):
        sums = [sums[m] + terms[j, m].astype(F32) for m in range(3)]
    gate, up, hgrad = sums
    sig = jax.nn.sigmoid(gate)
    out[0] = (hgrad * up * sig * (1.0 + gate * (1.0 - sig))).astype(BF16)
    out[1] = (hgrad * gate * sig).astype(BF16)
    out[2] = (gate * sig * up).astype(BF16)


def back_kernel(index, count, units, cols, gate, up, down, rows, grads, hidden, out_total, in_total):
    n_row, _, share, toks = units.shape
    for j in range(n_row):
        for m in range(3):
            hidden[m, j * share : (j + 1) * share, :] = units[j, m]
    out_total[...] = jnp.zeros_like(out_total)
    in_total[...] = jnp.zeros_like(in_total)
    grads[...] = jnp.zeros_like(grads)
    per = grads.shape[2]
    for m, weights in enumerate((gate, up, down)):
        side = m // 2
        total = out_total if m == 2 else in_total

        def step(s, live):
            block = jnp.where(live, weights[s], jnp.zeros_like(weights[s]))
            unit = hidden[m, rows_of(index[m, 1, s]), :]
            place = rows_of(index[m, 0, s])
            total[place, :] += jnp.dot(block, unit, preferred_element_type=F32)
            grad = lax.dot_general(
                cols[side, place, :], unit, (((1,), (1,)), ((), ())), preferred_element_type=F32
            )
            grad = jnp.where(live, grad, 0.0)
            packed = jnp.concatenate([grad[: BS // 2], grad[BS // 2 :]], axis=1)
            grads[s // per, m, s % per] = packed.astype(BF16)

        for_slots(count[m], step)
    n_col, pair, width = rows.shape
    half = pair // 2
    for j in range(0, width, 128):
        out_piece = out_total[j : j + 128, :].T.reshape(n_col, half, 128)
        in_piece = in_total[j : j + 128, :].T.reshape(n_col, half, 128)
        rows[:, :, j : j + 128] = jnp.concatenate([out_piece, in_piece], axis=1).astype(BF16)


def unpack_kernel(packed, gate, up, down, flat):
    n_dp, _, per, depth, lanes = packed.shape
    slots = n_dp * per
    low = lax.broadcasted_iota(jnp.int32, (slots, lanes), 1) < BS
    for m, out in enumerate((gate, up, down)):
        for g in range(n_dp):
            flat[g * per * depth : (g + 1) * per * depth, :] = (
                packed[g, m].astype(F32).reshape(per * depth, lanes)
            )
        for k in range(0, depth, 2):
            even = flat[pl.ds(k, slots, stride=depth), :]
            odd = flat[pl.ds(k + 1, slots, stride=depth), :]
            out[:, k * BS : k * BS + lanes] = jnp.where(low, even, pltpu.roll(odd, BS, 1)).astype(BF16)
            start = (depth + k) * BS
            out[:, start : start + lanes] = jnp.where(low, pltpu.roll(even, BS, 1), odd).astype(BF16)


def per_device(tokens, grad_out, gate_blocks, up_blocks, down_blocks, block_index, block_count):
    n_dp, n_row, n_col = (lax.axis_size(a) for a in ("dp", "row", "col"))
    slots = gate_blocks.shape[2]
    half, width = tokens.shape
    toks = half * n_col
    units = 28 * BS
    share = units // n_row
    index = block_index.reshape(3, 2, slots)
    count = block_count.reshape(3)
    weights = [w.reshape(slots, BS, BS) for w in (gate_blocks, up_blocks, down_blocks)]

    both = jnp.concatenate([tokens, grad_out], axis=0)
    wide = lax.all_gather(both, "col", axis=0)
    cols, parts = pl.pallas_call(
        spread_kernel,
        out_shape=(
            jax.ShapeDtypeStruct((2, width, toks), BF16),
            jax.ShapeDtypeStruct((n_row, 3, share, toks), BF16),
        ),
        in_specs=[SMEM, SMEM, VMEM, VMEM, VMEM, VMEM],
        out_specs=(VMEM, VMEM),
        scratch_shapes=[pltpu.VMEM((3, units, toks), F32)],
        compiler_params=PARAMS,
        name="spread",
    )(index, count, wide, *weights)
    terms = lax.all_to_all(parts, "row", 0, 0)
    own = pl.pallas_call(
        hidden_kernel,
        out_shape=jax.ShapeDtypeStruct((3, share, toks), BF16),
        in_specs=[VMEM],
        out_specs=VMEM,
        compiler_params=PARAMS,
        name="hidden",
    )(terms)
    all_units = lax.all_gather(own, "row", axis=0)
    rows, grads = pl.pallas_call(
        back_kernel,
        out_shape=(
            jax.ShapeDtypeStruct((n_col, 2 * half, width), BF16),
            jax.ShapeDtypeStruct((n_dp, 3, slots // n_dp, BS // 2, 2 * BS), BF16),
        ),
        in_specs=[SMEM, SMEM, VMEM, VMEM, VMEM, VMEM, VMEM],
        out_specs=(VMEM, VMEM),
        scratch_shapes=[
            pltpu.VMEM((3, units, toks), BF16),
            pltpu.VMEM((width, toks), F32),
            pltpu.VMEM((width, toks), F32),
        ],
        compiler_params=PARAMS,
        name="back",
    )(index, count, all_units, cols, *weights)
    row_terms = lax.all_to_all(rows, "col", 0, 0)
    grad_terms = lax.all_to_all(grads, "dp", 0, 0)
    grad_own = jnp.sum(grad_terms.astype(F32), axis=0).astype(BF16)
    grad_all = lax.all_gather(grad_own, "dp", axis=0)
    flat = jax.ShapeDtypeStruct((slots, BS * BS), BF16)
    block_grads = pl.pallas_call(
        unpack_kernel,
        out_shape=(flat, flat, flat),
        in_specs=[VMEM],
        out_specs=(VMEM, VMEM, VMEM),
        scratch_shapes=[pltpu.VMEM((slots * BS // 2, 2 * BS), F32)],
        compiler_params=PARAMS,
        name="unpack",
    )(grad_all)
    row_sum = jnp.sum(row_terms.astype(F32), axis=0).astype(BF16)
    return (row_sum[:half], row_sum[half:], *(b[None, None] for b in block_grads))


def solution(mesh):
    placed = (
        P(("dp", "col"), "row"),
        P(("dp", "col"), "row"),
        P("row", "col", None, None),
        P("row", "col", None, None),
        P("row", "col", None, None),
        P(None, "row", "col", None, None),
        P(None, "row", "col"),
    )
    return jax.shard_map(
        per_device,
        mesh=mesh,
        in_specs=placed,
        out_specs=(
            P(("dp", "col"), "row"),
            P(("dp", "col"), "row"),
            P("row", "col", None, None),
            P("row", "col", None, None),
            P("row", "col", None, None),
        ),
        check_vma=False,
    )
```

```python
import jax
import jax.numpy as jnp
from jax import lax
from jax.experimental import pallas as pl
from jax.experimental.pallas import tpu as pltpu
from jax.sharding import PartitionSpec as P

BS = 64
UNROLL = 4
VMEM = pl.BlockSpec(memory_space=pltpu.VMEM)
SMEM = pl.BlockSpec(memory_space=pltpu.SMEM)
PARAMS = pltpu.CompilerParams(vmem_limit_bytes=40 * 1024 * 1024)
F32 = jnp.float32
BF16 = jnp.bfloat16


def for_slots(count, step):
    def group(g, carry):
        for u in range(UNROLL):
            s = g * UNROLL + u
            step(s, s < count)
        return carry

    lax.fori_loop(0, (count + UNROLL - 1) // UNROLL, group, 0)


def rows_of(block):
    return pl.ds(pl.multiple_of(block * BS, BS), BS)


def feature_major(wide, cols):
    n_col, pair, width = wide.shape
    half = pair // 2
    toks = n_col * half
    for j in range(0, width, 128):
        piece = wide[:, :, j : j + 128].astype(F32).reshape(n_col, 2, half, 128)
        for side in range(2):
            cols[side, j : j + 128, :] = piece[:, side].reshape(toks, 128).T.astype(BF16)


def spread_terms(index, count, cols, weights, total, mats):
    total[...] = jnp.zeros_like(total)
    for i, m in enumerate(mats):

        def step(s, live):
            block = jnp.where(live, weights[i][s], jnp.zeros_like(weights[i][s]))
            source = cols[m // 2, rows_of(index[m, 0, s]), :]
            place = rows_of(index[m, 1, s])
            total[i, place, :] += lax.dot_general(
                block, source, (((0,), (0,)), ((), ())), preferred_element_type=F32
            )

        for_slots(count[m], step)


def split_shares(total, mine, theirs):
    core = lax.axis_index("row") % 2
    share = mine.shape[2]
    for x in range(mine.shape[0]):
        for i in range(mine.shape[1]):
            for out, side in ((mine, core), (theirs, 1 - core)):
                first = pl.multiple_of((2 * x + side) * share, 32)
                out[x, i] = total[i, pl.ds(first, share), :].astype(BF16)


def gate_up_kernel(index, count, wide, gate, up, cols, mine, theirs, total):
    feature_major(wide, cols)
    spread_terms(index, count, cols, (gate, up), total, (0, 1))
    split_shares(total, mine, theirs)


def hgrad_kernel(index, count, cols, down, mine, theirs, total):
    spread_terms(index, count, cols, (down,), total, (2,))
    split_shares(total, mine, theirs)


def pair_sum_kernel(mine_ab, mine_c, other_ab, other_c, out):
    out[:, :2] = (mine_ab[...].astype(F32) + other_ab[...].astype(F32)).astype(BF16)
    out[:, 2:] = (mine_c[...].astype(F32) + other_c[...].astype(F32)).astype(BF16)


def hidden_kernel(terms, out):
    sums = [terms[0, m].astype(F32) for m in range(3)]
    for j in range(1, terms.shape[0]):
        sums = [sums[m] + terms[j, m].astype(F32) for m in range(3)]
    gate, up, hgrad = sums
    sig = jax.nn.sigmoid(gate)
    units = (
        (hgrad * up * sig * (1.0 + gate * (1.0 - sig))).astype(BF16),
        (hgrad * gate * sig).astype(BF16),
        (gate * sig * up).astype(BF16),
    )
    for j in range(out.shape[0]):
        for m in range(3):
            out[j, m] = units[m]


def back_kernel(index, count, mine, theirs, gate, up, down, rows, units, out_total, in_total):
    core = lax.axis_index("row") % 2
    share = mine.shape[2]
    for x in range(mine.shape[0]):
        for m in range(3):
            for half, side in ((mine, core), (theirs, 1 - core)):
                first = pl.multiple_of((2 * x + side) * share, 32)
                units[m, pl.ds(first, share), :] = half[x, m]
    out_total[...] = jnp.zeros_like(out_total)
    in_total[...] = jnp.zeros_like(in_total)
    for m, weights in enumerate((gate, up, down)):
        total = out_total if m == 2 else in_total

        def step(s, live):
            block = jnp.where(live, weights[s], jnp.zeros_like(weights[s]))
            unit = units[m, rows_of(index[m, 1, s]), :]
            place = rows_of(index[m, 0, s])
            total[place, :] += jnp.dot(block, unit, preferred_element_type=F32)

        for_slots(count[m], step)
    n_col, pair, width = rows.shape
    half = pair // 2
    for j in range(0, width, 128):
        out_piece = out_total[j : j + 128, :].T.reshape(n_col, half, 128)
        in_piece = in_total[j : j + 128, :].T.reshape(n_col, half, 128)
        rows[:, :, j : j + 128] = jnp.concatenate([out_piece, in_piece], axis=1).astype(BF16)


def grads_kernel(index, count, units, cols, *outs):
    n_dp = len(outs)
    per = outs[0].shape[1]
    here = lax.axis_index("dp")

    def step(p, carry):
        for away, out in enumerate(outs):
            s = ((here + away) % n_dp) * per + p
            for m in range(3):
                unit = units[m, rows_of(index[m, 1, s]), :]
                source = cols[m // 2, rows_of(index[m, 0, s]), :]
                grad = lax.dot_general(
                    source, unit, (((1,), (1,)), ((), ())), preferred_element_type=F32
                )
                grad = jnp.where(s < count[m], grad, 0.0)
                packed = jnp.concatenate([grad[: BS // 2], grad[BS // 2 :]], axis=1)
                out[m, p] = packed.astype(BF16)
        return carry

    lax.fori_loop(0, per, step, 0)


def dp_sum_kernel(a, b, c, d, out):
    out[...] = (
        (a[...].astype(F32) + b[...].astype(F32)) + (c[...].astype(F32) + d[...].astype(F32))
    ).astype(BF16)


def unpack_kernel(*refs):
    *pieces, gate, up, down, flat = refs
    n_dp = len(pieces)
    _, per, depth, lanes = pieces[0].shape
    slots = n_dp * per
    here = lax.axis_index("dp")
    low = lax.broadcasted_iota(jnp.int32, (slots, lanes), 1) < BS
    for m, out in enumerate((gate, up, down)):
        for away, piece in enumerate(pieces):
            owner = (here + n_dp - away) % n_dp
            first = pl.multiple_of(owner * per * depth, 32)
            flat[pl.ds(first, per * depth), :] = piece[m].astype(F32).reshape(per * depth, lanes)
        for k in range(0, depth, 2):
            even = flat[pl.ds(k, slots, stride=depth), :]
            odd = flat[pl.ds(k + 1, slots, stride=depth), :]
            out[:, k * BS : k * BS + lanes] = jnp.where(low, even, pltpu.roll(odd, BS, 1)).astype(BF16)
            start = (depth + k) * BS
            out[:, start : start + lanes] = jnp.where(low, pltpu.roll(even, BS, 1), odd).astype(BF16)


def call(body, name, out_shape, n_scalars, n_arrays, scratch=()):
    many = isinstance(out_shape, (tuple, list))
    return pl.pallas_call(
        body,
        out_shape=out_shape,
        in_specs=[SMEM] * n_scalars + [VMEM] * n_arrays,
        out_specs=tuple(VMEM for _ in out_shape) if many else VMEM,
        scratch_shapes=list(scratch),
        compiler_params=PARAMS,
        name=name,
    )


def per_device(tokens, grad_out, gate_blocks, up_blocks, down_blocks, block_index, block_count):
    n_dp, n_row, n_col = (lax.axis_size(a) for a in ("dp", "row", "col"))
    slots = gate_blocks.shape[2]
    half, width = tokens.shape
    toks = half * n_col
    units = 28 * BS
    share = units // n_row
    chips = n_row // 2
    index = block_index.reshape(3, 2, slots)
    count = block_count.reshape(3)
    gate, up, down = (w.reshape(slots, BS, BS) for w in (gate_blocks, up_blocks, down_blocks))
    pair = [(i, i ^ 1) for i in range(n_row)]
    same_core = [[2 * x + k for x in range(chips)] for k in range(2)]

    def arr(*shape):
        return jax.ShapeDtypeStruct(shape, BF16)

    both = jnp.concatenate([tokens, grad_out], axis=0)
    wide = lax.all_to_all(jnp.broadcast_to(both[None], (n_col, 2 * half, width)), "col", 0, 0)
    cols, mine_ab, theirs_ab = call(
        gate_up_kernel,
        "gate_up",
        (arr(2, width, toks), arr(chips, 2, share, toks), arr(chips, 2, share, toks)),
        2,
        3,
        [pltpu.VMEM((2, units, toks), F32)],
    )(index, count, wide, gate, up)
    other_ab = lax.ppermute(theirs_ab, "row", pair)
    mine_c, theirs_c = call(
        hgrad_kernel,
        "hgrad",
        (arr(chips, 1, share, toks), arr(chips, 1, share, toks)),
        2,
        2,
        [pltpu.VMEM((1, units, toks), F32)],
    )(index, count, cols, down)
    other_c = lax.ppermute(theirs_c, "row", pair)
    terms = call(pair_sum_kernel, "pair_sum", arr(chips, 3, share, toks), 0, 4)(
        mine_ab, mine_c, other_ab, other_c
    )
    terms = lax.all_to_all(terms, "row", 0, 0, axis_index_groups=same_core)
    own = call(hidden_kernel, "hidden", arr(chips, 3, share, toks), 0, 1)(terms)
    mine = lax.all_to_all(own, "row", 0, 0, axis_index_groups=same_core)
    theirs = lax.ppermute(mine, "row", pair)
    rows, band = call(
        back_kernel,
        "back",
        (arr(n_col, 2 * half, width), arr(3, units, toks)),
        2,
        5,
        [pltpu.VMEM((width, toks), F32), pltpu.VMEM((width, toks), F32)],
    )(index, count, mine, theirs, gate, up, down)
    row_terms = lax.all_to_all(rows, "col", 0, 0)
    packed = arr(3, slots // n_dp, BS // 2, 2 * BS)
    grads = call(grads_kernel, "grads", (packed,) * n_dp, 2, 2)(index, count, band, cols)
    moves = [[(i, (i + away) % n_dp) for i in range(n_dp)] for away in range(n_dp)]
    arrived = [lax.ppermute(grads[away], "dp", moves[away]) for away in range(1, n_dp)]
    summed = call(dp_sum_kernel, "dp_sum", packed, 0, n_dp)(grads[0], *arrived)
    pieces = [summed] + [lax.ppermute(summed, "dp", moves[away]) for away in range(1, n_dp)]
    flat = arr(slots, BS * BS)
    block_grads = call(
        unpack_kernel,
        "unpack",
        (flat, flat, flat),
        0,
        n_dp,
        [pltpu.VMEM((slots * BS // 2, 2 * BS), F32)],
    )(*pieces)
    row_sum = jnp.sum(row_terms.astype(F32), axis=0).astype(BF16)
    return (row_sum[:half], row_sum[half:], *(b[None, None] for b in block_grads))


def solution(mesh):
    placed = (
        P(("dp", "col"), "row"),
        P(("dp", "col"), "row"),
        P("row", "col", None, None),
        P("row", "col", None, None),
        P("row", "col", None, None),
        P(None, "row", "col", None, None),
        P(None, "row", "col"),
    )
    return jax.shard_map(
        per_device,
        mesh=mesh,
        in_specs=placed,
        out_specs=(
            P(("dp", "col"), "row"),
            P(("dp", "col"), "row"),
            P("row", "col", None, None),
            P("row", "col", None, None),
            P("row", "col", None, None),
        ),
        check_vma=False,
    )
```

```python
import jax
import jax.numpy as jnp
from jax import lax
from jax.experimental import pallas as pl
from jax.experimental.pallas import tpu as pltpu
from jax.sharding import PartitionSpec as P

BS = 64
UNROLL = 4
VMEM = pl.BlockSpec(memory_space=pltpu.VMEM)
SMEM = pl.BlockSpec(memory_space=pltpu.SMEM)
PARAMS = pltpu.CompilerParams(vmem_limit_bytes=40 * 1024 * 1024)
F32 = jnp.float32
BF16 = jnp.bfloat16


def for_slots(count, step):
    def group(g, carry):
        for u in range(UNROLL):
            s = g * UNROLL + u
            step(s, s < count)
        return carry

    lax.fori_loop(0, (count + UNROLL - 1) // UNROLL, group, 0)


def rows_of(block):
    return pl.ds(pl.multiple_of(block * BS, BS), BS)


def feature_major(wide, cols):
    n_col, pair, width = wide.shape
    half = pair // 2
    toks = n_col * half
    for j in range(0, width, 128):
        piece = wide[:, :, j : j + 128].astype(F32).reshape(n_col, 2, half, 128)
        for side in range(2):
            cols[side, j : j + 128, :] = piece[:, side].reshape(toks, 128).T.astype(BF16)


def spread_kernel(index, count, wide, gate, up, down, cols, mine, theirs, total):
    feature_major(wide, cols)
    total[...] = jnp.zeros_like(total)
    for m, weights in enumerate((gate, up, down)):

        def step(s, live):
            block = jnp.where(live, weights[s], jnp.zeros_like(weights[s]))
            source = cols[m // 2, rows_of(index[m, 0, s]), :]
            place = rows_of(index[m, 1, s])
            total[m, place, :] += lax.dot_general(
                block, source, (((0,), (0,)), ((), ())), preferred_element_type=F32
            )

        for_slots(count[m], step)
    core = lax.axis_index("row") % 2
    share = mine.shape[2]
    for x in range(mine.shape[0]):
        for m in range(3):
            for out, side in ((theirs, 1 - core), (mine, core)):
                first = pl.multiple_of((2 * x + side) * share, 32)
                out[x, m] = total[m, pl.ds(first, share), :].astype(BF16)


def pair_sum_kernel(mine, other, out):
    out[...] = (mine[...].astype(F32) + other[...].astype(F32)).astype(BF16)


def hidden_kernel(terms, out):
    sums = [terms[0, m].astype(F32) for m in range(3)]
    for j in range(1, terms.shape[0]):
        sums = [sums[m] + terms[j, m].astype(F32) for m in range(3)]
    gate, up, hgrad = sums
    sig = jax.nn.sigmoid(gate)
    units = (
        (hgrad * up * sig * (1.0 + gate * (1.0 - sig))).astype(BF16),
        (hgrad * gate * sig).astype(BF16),
        (gate * sig * up).astype(BF16),
    )
    for j in range(out.shape[0]):
        for m in range(3):
            out[j, m] = units[m]


def grads_kernel(index, count, mine, theirs, cols, band, own, ahead, across, behind):
    core = lax.axis_index("row") % 2
    share = mine.shape[2]
    for x in range(mine.shape[0]):
        for m in range(3):
            for half, side in ((mine, core), (theirs, 1 - core)):
                first = pl.multiple_of((2 * x + side) * share, 32)
                band[m, pl.ds(first, share), :] = half[x, m]
    outs = (own, ahead, across, behind)
    n_dp = len(outs)
    per = own.shape[1]
    here = lax.axis_index("dp")

    def step(p, carry):
        for away, out in enumerate(outs):
            s = ((here + away) % n_dp) * per + p
            for m in range(3):
                unit = band[m, rows_of(index[m, 1, s]), :]
                source = cols[m // 2, rows_of(index[m, 0, s]), :]
                grad = lax.dot_general(
                    source, unit, (((1,), (1,)), ((), ())), preferred_element_type=F32
                )
                grad = jnp.where(s < count[m], grad, 0.0)
                packed = jnp.concatenate([grad[: BS // 2], grad[BS // 2 :]], axis=1)
                out[m, p] = packed.astype(BF16)
        return carry

    lax.fori_loop(0, per, step, 0)


def back_kernel(index, count, band, gate, up, down, rows, out_total, in_total):
    out_total[...] = jnp.zeros_like(out_total)
    in_total[...] = jnp.zeros_like(in_total)
    for m, weights in enumerate((gate, up, down)):
        total = out_total if m == 2 else in_total

        def step(s, live):
            block = jnp.where(live, weights[s], jnp.zeros_like(weights[s]))
            unit = band[m, rows_of(index[m, 1, s]), :]
            place = rows_of(index[m, 0, s])
            total[place, :] += jnp.dot(block, unit, preferred_element_type=F32)

        for_slots(count[m], step)
    n_col, pair, width = rows.shape
    half = pair // 2
    for j in range(0, width, 128):
        out_piece = out_total[j : j + 128, :].T.reshape(n_col, half, 128)
        in_piece = in_total[j : j + 128, :].T.reshape(n_col, half, 128)
        rows[:, :, j : j + 128] = jnp.concatenate([out_piece, in_piece], axis=1).astype(BF16)


def dp_sum_kernel(a, b, c, d, out):
    out[...] = (
        (a[...].astype(F32) + b[...].astype(F32)) + (c[...].astype(F32) + d[...].astype(F32))
    ).astype(BF16)


def unpack_kernel(own, prev, next_, far_low, far_high, gate, up, down, flat):
    n_dp = 4
    _, per, depth, lanes = own.shape
    slots = n_dp * per
    here = lax.axis_index("dp")
    low = lax.broadcasted_iota(jnp.int32, (slots, lanes), 1) < BS
    for m, out in enumerate((gate, up, down)):
        for away, piece in ((0, own[m]), (3, prev[m]), (1, next_[m]), (2, None)):
            if piece is None:
                piece = jnp.concatenate([far_low[m], far_high[m]], axis=1)
            first = pl.multiple_of(((here + away) % n_dp) * per * depth, 32)
            flat[pl.ds(first, per * depth), :] = piece.astype(F32).reshape(per * depth, lanes)
        for k in range(0, depth, 2):
            even = flat[pl.ds(k, slots, stride=depth), :]
            odd = flat[pl.ds(k + 1, slots, stride=depth), :]
            out[:, k * BS : k * BS + lanes] = jnp.where(low, even, pltpu.roll(odd, BS, 1)).astype(BF16)
            start = (depth + k) * BS
            out[:, start : start + lanes] = jnp.where(low, pltpu.roll(even, BS, 1), odd).astype(BF16)


def call(body, name, out_shape, ins, outs, scratch=()):
    return pl.pallas_call(
        body,
        out_shape=out_shape,
        in_specs=ins,
        out_specs=outs,
        scratch_shapes=list(scratch),
        compiler_params=PARAMS,
        name=name,
    )


def per_device(tokens, grad_out, gate_blocks, up_blocks, down_blocks, block_index, block_count):
    n_dp, n_row, n_col = (lax.axis_size(a) for a in ("dp", "row", "col"))
    slots = gate_blocks.shape[2]
    half, width = tokens.shape
    toks = half * n_col
    units = 28 * BS
    share = units // n_row
    chips = n_row // 2
    index = block_index.reshape(3, 2, slots)
    count = block_count.reshape(3)
    gate, up, down = (w.reshape(slots, BS, BS) for w in (gate_blocks, up_blocks, down_blocks))
    pair = [(i, i ^ 1) for i in range(n_row)]
    same_core = [[2 * x + k for x in range(chips)] for k in range(2)]
    ahead, behind, across = ([(i, (i + d) % n_dp) for i in range(n_dp)] for d in (1, 3, 2))

    def arr(*shape):
        return jax.ShapeDtypeStruct(shape, BF16)

    both = jnp.concatenate([tokens, grad_out], axis=0)
    wide = lax.all_gather(both, "col", axis=0)
    terms = arr(chips, 3, share, toks)
    cols, mine, theirs = call(
        spread_kernel,
        "spread",
        (arr(2, width, toks), terms, terms),
        [SMEM] * 2 + [VMEM] * 4,
        (VMEM,) * 3,
        [pltpu.VMEM((3, units, toks), F32)],
    )(index, count, wide, gate, up, down)
    other = lax.ppermute(theirs, "row", pair)
    paired = call(pair_sum_kernel, "pair_sum", terms, [VMEM] * 2, VMEM)(mine, other)
    summed = lax.all_to_all(paired, "row", 0, 0, axis_index_groups=same_core)
    own = call(hidden_kernel, "hidden", terms, [VMEM], VMEM)(summed)
    mine = lax.all_to_all(own, "row", 0, 0, axis_index_groups=same_core)
    theirs = lax.ppermute(mine, "row", pair)
    packed = arr(3, slots // n_dp, BS // 2, 2 * BS)
    band, own, to_next, to_far, to_prev = call(
        grads_kernel,
        "grads",
        (arr(3, units, toks),) + (packed,) * n_dp,
        [SMEM] * 2 + [VMEM] * 3,
        (VMEM,) * (1 + n_dp),
    )(index, count, mine, theirs, cols)
    rows = call(
        back_kernel,
        "back",
        arr(n_col, 2 * half, width),
        [SMEM] * 2 + [VMEM] * 4,
        VMEM,
        [pltpu.VMEM((width, toks), F32), pltpu.VMEM((width, toks), F32)],
    )(index, count, band, gate, up, down)
    row_terms = lax.all_to_all(rows, "col", 0, 0)
    from_far = lax.ppermute(to_far, "dp", across)
    from_prev = lax.ppermute(to_next, "dp", ahead)
    from_next = lax.ppermute(to_prev, "dp", behind)
    own = call(dp_sum_kernel, "dp_sum", packed, [VMEM] * 4, VMEM)(own, from_far, from_prev, from_next)
    prev = lax.ppermute(own, "dp", ahead)
    next_ = lax.ppermute(own, "dp", behind)
    cut = BS // 4
    far_low = lax.ppermute(prev[:, :, :cut], "dp", ahead)
    far_high = lax.ppermute(next_[:, :, cut:], "dp", behind)
    flat = arr(slots, BS * BS)
    block_grads = call(
        unpack_kernel,
        "unpack",
        (flat, flat, flat),
        [VMEM] * 5,
        (VMEM,) * 3,
        [pltpu.VMEM((slots * BS // 2, 2 * BS), F32)],
    )(own, prev, next_, far_low, far_high)
    row_sum = jnp.sum(row_terms.astype(F32), axis=0).astype(BF16)
    return (row_sum[:half], row_sum[half:], *(b[None, None] for b in block_grads))


def solution(mesh):
    placed = (
        P(("dp", "col"), "row"),
        P(("dp", "col"), "row"),
        P("row", "col", None, None),
        P("row", "col", None, None),
        P("row", "col", None, None),
        P(None, "row", "col", None, None),
        P(None, "row", "col"),
    )
    return jax.shard_map(
        per_device,
        mesh=mesh,
        in_specs=placed,
        out_specs=(
            P(("dp", "col"), "row"),
            P(("dp", "col"), "row"),
            P("row", "col", None, None),
            P("row", "col", None, None),
            P("row", "col", None, None),
        ),
        check_vma=False,
    )
```

```python
import jax
import jax.numpy as jnp
from jax import lax
from jax.experimental import pallas as pl
from jax.experimental.pallas import tpu as pltpu
from jax.sharding import PartitionSpec as P

BS = 64
UNROLL = 4
VMEM = pl.BlockSpec(memory_space=pltpu.VMEM)
SMEM = pl.BlockSpec(memory_space=pltpu.SMEM)
PARAMS = pltpu.CompilerParams(vmem_limit_bytes=40 * 1024 * 1024)
F32 = jnp.float32
BF16 = jnp.bfloat16


def for_slots(count, step):
    def group(g, carry):
        for u in range(UNROLL):
            s = g * UNROLL + u
            step(s, s < count)
        return carry

    lax.fori_loop(0, (count + UNROLL - 1) // UNROLL, group, 0)


def rows_of(block):
    return pl.ds(pl.multiple_of(block * BS, BS), BS)


def feature_major(wide, cols):
    n_col, pair, width = wide.shape
    half = pair // 2
    toks = n_col * half
    for j in range(0, width, 128):
        piece = wide[:, :, j : j + 128].astype(F32).reshape(n_col, 2, half, 128)
        for side in range(2):
            cols[side, j : j + 128, :] = piece[:, side].reshape(toks, 128).T.astype(BF16)


def spread_kernel(index, count, wide, gate, up, down, cols, mine, theirs, total):
    feature_major(wide, cols)
    total[...] = jnp.zeros_like(total)
    for m, weights in enumerate((gate, up, down)):

        def step(s, live):
            block = jnp.where(live, weights[s], jnp.zeros_like(weights[s]))
            source = cols[m // 2, rows_of(index[m, 0, s]), :]
            place = rows_of(index[m, 1, s])
            total[m, place, :] += lax.dot_general(
                block, source, (((0,), (0,)), ((), ())), preferred_element_type=F32
            )

        for_slots(count[m], step)
    core = lax.axis_index("row") % 2
    share = mine.shape[2]
    for x in range(mine.shape[0]):
        for m in range(3):
            for out, side in ((theirs, 1 - core), (mine, core)):
                first = pl.multiple_of((2 * x + side) * share, 32)
                out[x, m] = total[m, pl.ds(first, share), :].astype(BF16)


def pair_sum_kernel(mine, other, out):
    out[...] = (mine[...].astype(F32) + other[...].astype(F32)).astype(BF16)


def hidden_kernel(terms, out):
    sums = [terms[0, m].astype(F32) for m in range(3)]
    for j in range(1, terms.shape[0]):
        sums = [sums[m] + terms[j, m].astype(F32) for m in range(3)]
    gate, up, hgrad = sums
    sig = jax.nn.sigmoid(gate)
    units = (
        (hgrad * up * sig * (1.0 + gate * (1.0 - sig))).astype(BF16),
        (hgrad * gate * sig).astype(BF16),
        (gate * sig * up).astype(BF16),
    )
    for j in range(out.shape[0]):
        for m in range(3):
            out[j, m] = units[m]


def grads_kernel(index, count, mine, theirs, cols, band, grads):
    core = lax.axis_index("row") % 2
    share = mine.shape[2]
    for x in range(mine.shape[0]):
        for m in range(3):
            for half, side in ((mine, core), (theirs, 1 - core)):
                first = pl.multiple_of((2 * x + side) * share, 32)
                band[m, pl.ds(first, share), :] = half[x, m]
    n_dp, _, per = grads.shape[:3]

    def step(p, carry):
        for owner in range(n_dp):
            s = owner * per + p
            for m in range(3):
                unit = band[m, rows_of(index[m, 1, s]), :]
                source = cols[m // 2, rows_of(index[m, 0, s]), :]
                grad = lax.dot_general(
                    source, unit, (((1,), (1,)), ((), ())), preferred_element_type=F32
                )
                grad = jnp.where(s < count[m], grad, 0.0)
                packed = jnp.concatenate([grad[: BS // 2], grad[BS // 2 :]], axis=1)
                grads[owner, m, p] = packed.astype(BF16)
        return carry

    lax.fori_loop(0, per, step, 0)


def back_kernel(index, count, band, gate, up, down, keep, give, out_total, in_total):
    out_total[...] = jnp.zeros_like(out_total)
    in_total[...] = jnp.zeros_like(in_total)
    for m, weights in enumerate((gate, up, down)):
        total = out_total if m == 2 else in_total

        def step(s, live):
            block = jnp.where(live, weights[s], jnp.zeros_like(weights[s]))
            unit = band[m, rows_of(index[m, 1, s]), :]
            place = rows_of(index[m, 0, s])
            total[place, :] += jnp.dot(block, unit, preferred_element_type=F32)

        for_slots(count[m], step)
    even_here = lax.axis_index("col") % 2 == 0
    owners, pair, width = keep.shape
    half = pair // 2
    for j in range(0, width, 128):
        out_piece = out_total[j : j + 128, :].T.reshape(owners, 2, half, 128)
        in_piece = in_total[j : j + 128, :].T.reshape(owners, 2, half, 128)
        piece = jnp.concatenate([out_piece, in_piece], axis=2)
        even, odd = piece[:, 0], piece[:, 1]
        keep[:, :, j : j + 128] = jnp.where(even_here, even, odd).astype(BF16)
        give[:, :, j : j + 128] = jnp.where(even_here, odd, even).astype(BF16)


def dp_sum_kernel(terms, out):
    out[...] = (
        (terms[0].astype(F32) + terms[1].astype(F32)) + (terms[2].astype(F32) + terms[3].astype(F32))
    ).astype(BF16)


def unpack_kernel(own, prev, next_, far_low, far_high, gate, up, down, flat):
    n_dp = 4
    _, per, depth, lanes = own.shape
    slots = n_dp * per
    here = lax.axis_index("dp")
    low = lax.broadcasted_iota(jnp.int32, (slots, lanes), 1) < BS
    for m, out in enumerate((gate, up, down)):
        for away, piece in ((0, own[m]), (3, prev[m]), (1, next_[m]), (2, None)):
            if piece is None:
                piece = jnp.concatenate([far_low[m], far_high[m]], axis=1)
            first = pl.multiple_of(((here + away) % n_dp) * per * depth, 32)
            flat[pl.ds(first, per * depth), :] = piece.astype(F32).reshape(per * depth, lanes)
        for k in range(0, depth, 2):
            even = flat[pl.ds(k, slots, stride=depth), :]
            odd = flat[pl.ds(k + 1, slots, stride=depth), :]
            out[:, k * BS : k * BS + lanes] = jnp.where(low, even, pltpu.roll(odd, BS, 1)).astype(BF16)
            start = (depth + k) * BS
            out[:, start : start + lanes] = jnp.where(low, pltpu.roll(even, BS, 1), odd).astype(BF16)


def call(body, name, out_shape, ins, outs, scratch=()):
    return pl.pallas_call(
        body,
        out_shape=out_shape,
        in_specs=ins,
        out_specs=outs,
        scratch_shapes=list(scratch),
        compiler_params=PARAMS,
        name=name,
    )


def per_device(tokens, grad_out, gate_blocks, up_blocks, down_blocks, block_index, block_count):
    n_dp, n_row, n_col = (lax.axis_size(a) for a in ("dp", "row", "col"))
    slots = gate_blocks.shape[2]
    half, width = tokens.shape
    toks = half * n_col
    units = 28 * BS
    share = units // n_row
    chips = n_row // 2
    index = block_index.reshape(3, 2, slots)
    count = block_count.reshape(3)
    gate, up, down = (w.reshape(slots, BS, BS) for w in (gate_blocks, up_blocks, down_blocks))
    pair = [(i, i ^ 1) for i in range(n_row)]
    same_core = [[2 * x + k for x in range(chips)] for k in range(2)]
    ahead, behind, across = ([(i, (i + d) % n_dp) for i in range(n_dp)] for d in (1, 3, 2))

    def arr(*shape):
        return jax.ShapeDtypeStruct(shape, BF16)

    both = jnp.concatenate([tokens, grad_out], axis=0)
    wide = lax.all_gather(both, "col", axis=0)
    terms = arr(chips, 3, share, toks)
    cols, mine, theirs = call(
        spread_kernel,
        "spread",
        (arr(2, width, toks), terms, terms),
        [SMEM] * 2 + [VMEM] * 4,
        (VMEM,) * 3,
        [pltpu.VMEM((3, units, toks), F32)],
    )(index, count, wide, gate, up, down)
    other = lax.ppermute(theirs, "row", pair)
    paired = call(pair_sum_kernel, "pair_sum", terms, [VMEM] * 2, VMEM)(mine, other)
    summed = lax.all_to_all(paired, "row", 0, 0, axis_index_groups=same_core)
    own = call(hidden_kernel, "hidden", terms, [VMEM], VMEM)(summed)
    mine = lax.all_to_all(own, "row", 0, 0, axis_index_groups=same_core)
    theirs = lax.ppermute(mine, "row", pair)
    packed = arr(3, slots // n_dp, BS // 2, 2 * BS)
    band, grads = call(
        grads_kernel,
        "grads",
        (arr(3, units, toks), arr(n_dp, *packed.shape)),
        [SMEM] * 2 + [VMEM] * 3,
        (VMEM, VMEM),
    )(index, count, mine, theirs, cols)
    grad_terms = lax.all_to_all(grads, "dp", 0, 0)
    row_half = arr(n_col // 2, 2 * half, width)
    keep, give = call(
        back_kernel,
        "back",
        (row_half, row_half),
        [SMEM] * 2 + [VMEM] * 4,
        (VMEM, VMEM),
        [pltpu.VMEM((width, toks), F32), pltpu.VMEM((width, toks), F32)],
    )(index, count, band, gate, up, down)
    given = lax.ppermute(give, "col", [(i, i ^ 1) for i in range(n_col)])
    halved = call(pair_sum_kernel, "col_pair_sum", row_half, [VMEM] * 2, VMEM)(keep, given)
    own = call(dp_sum_kernel, "dp_sum", packed, [VMEM], VMEM)(grad_terms)
    same_parity = [list(range(p, n_col, 2)) for p in range(2)]
    row_terms = lax.all_to_all(halved, "col", 0, 0, axis_index_groups=same_parity)
    prev = lax.ppermute(own, "dp", ahead)
    next_ = lax.ppermute(own, "dp", behind)
    cut = BS // 4
    far_low = lax.ppermute(prev[:, :, :cut], "dp", ahead)
    far_high = lax.ppermute(next_[:, :, cut:], "dp", behind)
    flat = arr(slots, BS * BS)
    block_grads = call(
        unpack_kernel,
        "unpack",
        (flat, flat, flat),
        [VMEM] * 5,
        (VMEM,) * 3,
        [pltpu.VMEM((slots * BS // 2, 2 * BS), F32)],
    )(own, prev, next_, far_low, far_high)
    row_sum = jnp.sum(row_terms.astype(F32), axis=0).astype(BF16)
    return (row_sum[:half], row_sum[half:], *(b[None, None] for b in block_grads))


def solution(mesh):
    placed = (
        P(("dp", "col"), "row"),
        P(("dp", "col"), "row"),
        P("row", "col", None, None),
        P("row", "col", None, None),
        P("row", "col", None, None),
        P(None, "row", "col", None, None),
        P(None, "row", "col"),
    )
    return jax.shard_map(
        per_device,
        mesh=mesh,
        in_specs=placed,
        out_specs=(
            P(("dp", "col"), "row"),
            P(("dp", "col"), "row"),
            P("row", "col", None, None),
            P("row", "col", None, None),
            P("row", "col", None, None),
        ),
        check_vma=False,
    )
```

```python
import jax
import jax.numpy as jnp
from jax import lax
from jax.experimental import pallas as pl
from jax.experimental.pallas import tpu as pltpu
from jax.sharding import PartitionSpec as P

BS = 64
UNROLL = 4
REST = 8
VMEM = pl.BlockSpec(memory_space=pltpu.VMEM)
SMEM = pl.BlockSpec(memory_space=pltpu.SMEM)
PARAMS = pltpu.CompilerParams(vmem_limit_bytes=40 * 1024 * 1024)
F32 = jnp.float32
BF16 = jnp.bfloat16


def for_slots(count, step):
    def group(g, carry):
        for u in range(UNROLL):
            s = g * UNROLL + u
            step(s, s < count)
        return carry

    lax.fori_loop(0, (count + UNROLL - 1) // UNROLL, group, 0)


def rows_of(block):
    return pl.ds(pl.multiple_of(block * BS, BS), BS)


def feature_major(wide, cols):
    n_col, pair, width = wide.shape
    half = pair // 2
    toks = n_col * half
    for j in range(0, width, 128):
        piece = wide[:, :, j : j + 128].astype(F32).reshape(n_col, 2, half, 128)
        for side in range(2):
            cols[side, j : j + 128, :] = piece[:, side].reshape(toks, 128).T.astype(BF16)


def spread_kernel(index, count, wide, gate, up, down, cols, mine, theirs, total):
    feature_major(wide, cols)
    total[...] = jnp.zeros_like(total)
    for m, weights in enumerate((gate, up, down)):

        def step(s, live):
            block = jnp.where(live, weights[s], jnp.zeros_like(weights[s]))
            source = cols[m // 2, rows_of(index[m, 0, s]), :]
            place = rows_of(index[m, 1, s])
            total[m, place, :] += lax.dot_general(
                block, source, (((0,), (0,)), ((), ())), preferred_element_type=F32
            )

        for_slots(count[m], step)
    core = lax.axis_index("row") % 2
    share = mine.shape[2]
    for x in range(mine.shape[0]):
        for m in range(3):
            for out, side in ((theirs, 1 - core), (mine, core)):
                first = pl.multiple_of((2 * x + side) * share, 32)
                out[x, m] = total[m, pl.ds(first, share), :].astype(BF16)


def pair_sum_kernel(mine, other, out):
    out[...] = (mine[...].astype(F32) + other[...].astype(F32)).astype(BF16)


def hidden_kernel(terms, out):
    sums = [terms[0, m].astype(F32) for m in range(3)]
    for j in range(1, terms.shape[0]):
        sums = [sums[m] + terms[j, m].astype(F32) for m in range(3)]
    gate, up, hgrad = sums
    sig = jax.nn.sigmoid(gate)
    units = (
        (hgrad * up * sig * (1.0 + gate * (1.0 - sig))).astype(BF16),
        (hgrad * gate * sig).astype(BF16),
        (gate * sig * up).astype(BF16),
    )
    for j in range(out.shape[0]):
        for m in range(3):
            out[j, m] = units[m]


def grads_kernel(index, count, mine, theirs, cols, band, own, ahead, across, behind):
    core = lax.axis_index("row") % 2
    share = mine.shape[2]
    for x in range(mine.shape[0]):
        for m in range(3):
            for half, side in ((mine, core), (theirs, 1 - core)):
                first = pl.multiple_of((2 * x + side) * share, 32)
                band[m, pl.ds(first, share), :] = half[x, m]
    outs = (own, ahead, across, behind)
    n_dp = len(outs)
    rest = REST
    per = own.shape[0] - rest
    slots = index.shape[2]
    here = lax.axis_index("dp")

    def packed(q):
        m, s = q // slots, q % slots
        unit = band[m, rows_of(index[m, 1, s]), :]
        source = cols[m // 2, rows_of(index[m, 0, s]), :]
        grad = lax.dot_general(source, unit, (((1,), (1,)), ((), ())), preferred_element_type=F32)
        grad = jnp.where(s < count[m], grad, 0.0)
        return jnp.concatenate([grad[: BS // 2], grad[BS // 2 :]], axis=1).astype(BF16)

    def step(p, carry):
        for away, out in enumerate(outs):
            out[p] = packed(((here + away) % n_dp) * per + p)
        return carry

    lax.fori_loop(0, per, step, 0, unroll=2)
    for p in range(rest):
        left = packed(n_dp * per + p)
        for out in outs:
            out[per + p] = left


def back_kernel(index, count, band, gate, up, down, rows, out_total, in_total):
    out_total[...] = jnp.zeros_like(out_total)
    in_total[...] = jnp.zeros_like(in_total)
    for m, weights in enumerate((gate, up, down)):
        total = out_total if m == 2 else in_total

        def step(s, live):
            block = jnp.where(live, weights[s], jnp.zeros_like(weights[s]))
            unit = band[m, rows_of(index[m, 1, s]), :]
            place = rows_of(index[m, 0, s])
            total[place, :] += jnp.dot(block, unit, preferred_element_type=F32)

        for_slots(count[m], step)
    n_col, pair, width = rows.shape
    half = pair // 2
    for j in range(0, width, 128):
        out_piece = out_total[j : j + 128, :].T.reshape(n_col, half, 128)
        in_piece = in_total[j : j + 128, :].T.reshape(n_col, half, 128)
        rows[:, :, j : j + 128] = jnp.concatenate([out_piece, in_piece], axis=1).astype(BF16)


def dp_sum_kernel(here, far, prev, next_, own, rest):
    total = (here[...].astype(F32) + far[...].astype(F32)) + (
        prev[...].astype(F32) + next_[...].astype(F32)
    )
    own[...] = total[: own.shape[0]].astype(BF16)
    rest[...] = total[own.shape[0] :].astype(BF16)


def unpack_kernel(owned, rest, gate, up, down, flat):
    n_dp, per, depth, lanes = owned.shape
    slots = gate.shape[0]
    low = lax.broadcasted_iota(jnp.int32, (slots, lanes), 1) < BS
    for g in range(n_dp):
        flat[g * per * depth : (g + 1) * per * depth, :] = (
            owned[g].astype(F32).reshape(per * depth, lanes)
        )
    flat[n_dp * per * depth :, :] = rest[...].astype(F32).reshape(-1, lanes)
    for m, out in enumerate((gate, up, down)):
        base = m * slots * depth
        for k in range(0, depth, 2):
            even = flat[pl.ds(base + k, slots, stride=depth), :]
            odd = flat[pl.ds(base + k + 1, slots, stride=depth), :]
            out[:, k * BS : k * BS + lanes] = jnp.where(low, even, pltpu.roll(odd, BS, 1)).astype(BF16)
            start = (depth + k) * BS
            out[:, start : start + lanes] = jnp.where(low, pltpu.roll(even, BS, 1), odd).astype(BF16)


def call(body, name, out_shape, ins, outs, scratch=()):
    return pl.pallas_call(
        body,
        out_shape=out_shape,
        in_specs=ins,
        out_specs=outs,
        scratch_shapes=list(scratch),
        compiler_params=PARAMS,
        name=name,
    )


def per_device(tokens, grad_out, gate_blocks, up_blocks, down_blocks, block_index, block_count):
    n_dp, n_row, n_col = (lax.axis_size(a) for a in ("dp", "row", "col"))
    slots = gate_blocks.shape[2]
    half, width = tokens.shape
    toks = half * n_col
    units = 28 * BS
    share = units // n_row
    chips = n_row // 2
    index = block_index.reshape(3, 2, slots)
    count = block_count.reshape(3)
    gate, up, down = (w.reshape(slots, BS, BS) for w in (gate_blocks, up_blocks, down_blocks))
    pair = [(i, i ^ 1) for i in range(n_row)]
    same_core = [[2 * x + k for x in range(chips)] for k in range(2)]
    ahead, behind, across = ([(i, (i + d) % n_dp) for i in range(n_dp)] for d in (1, 3, 2))

    def arr(*shape):
        return jax.ShapeDtypeStruct(shape, BF16)

    both = jnp.concatenate([tokens, grad_out], axis=0)
    wide = lax.all_gather(both, "col", axis=0)
    terms = arr(chips, 3, share, toks)
    cols, mine, theirs = call(
        spread_kernel,
        "spread",
        (arr(2, width, toks), terms, terms),
        [SMEM] * 2 + [VMEM] * 4,
        (VMEM,) * 3,
        [pltpu.VMEM((3, units, toks), F32)],
    )(index, count, wide, gate, up, down)
    other = lax.ppermute(theirs, "row", pair)
    paired = call(pair_sum_kernel, "pair_sum", terms, [VMEM] * 2, VMEM)(mine, other)
    summed = lax.all_to_all(paired, "row", 0, 0, axis_index_groups=same_core)
    own = call(hidden_kernel, "hidden", terms, [VMEM], VMEM)(summed)
    mine = lax.all_to_all(own, "row", 0, 0, axis_index_groups=same_core)
    theirs = lax.ppermute(mine, "row", pair)
    per = (3 * slots - REST) // n_dp
    packed = arr(per + REST, BS // 2, 2 * BS)
    band, own, to_next, to_far, to_prev = call(
        grads_kernel,
        "grads",
        (arr(3, units, toks),) + (packed,) * n_dp,
        [SMEM] * 2 + [VMEM] * 3,
        (VMEM,) * (1 + n_dp),
    )(index, count, mine, theirs, cols)
    rows = call(
        back_kernel,
        "back",
        arr(n_col, 2 * half, width),
        [SMEM] * 2 + [VMEM] * 4,
        VMEM,
        [pltpu.VMEM((width, toks), F32), pltpu.VMEM((width, toks), F32)],
    )(index, count, band, gate, up, down)
    row_terms = lax.all_to_all(rows, "col", 0, 0)
    from_far = lax.ppermute(to_far, "dp", across)
    from_prev = lax.ppermute(to_next, "dp", ahead)
    from_next = lax.ppermute(to_prev, "dp", behind)
    own, rest = call(
        dp_sum_kernel,
        "dp_sum",
        (arr(per, BS // 2, 2 * BS), arr(REST, BS // 2, 2 * BS)),
        [VMEM] * 4,
        (VMEM,) * 2,
    )(own, from_far, from_prev, from_next)
    owned = lax.all_gather(own, "dp", axis=0)
    flat = arr(slots, BS * BS)
    block_grads = call(
        unpack_kernel,
        "unpack",
        (flat, flat, flat),
        [VMEM] * 2,
        (VMEM,) * 3,
        [pltpu.VMEM((3 * slots * BS // 2, 2 * BS), F32)],
    )(owned, rest)
    row_sum = jnp.sum(row_terms.astype(F32), axis=0).astype(BF16)
    return (row_sum[:half], row_sum[half:], *(b[None, None] for b in block_grads))


def solution(mesh):
    placed = (
        P(("dp", "col"), "row"),
        P(("dp", "col"), "row"),
        P("row", "col", None, None),
        P("row", "col", None, None),
        P("row", "col", None, None),
        P(None, "row", "col", None, None),
        P(None, "row", "col"),
    )
    return jax.shard_map(
        per_device,
        mesh=mesh,
        in_specs=placed,
        out_specs=(
            P(("dp", "col"), "row"),
            P(("dp", "col"), "row"),
            P("row", "col", None, None),
            P("row", "col", None, None),
            P("row", "col", None, None),
        ),
        check_vma=False,
    )
```

```python
import jax
import jax.numpy as jnp
from jax import lax
from jax.experimental import pallas as pl
from jax.experimental.pallas import tpu as pltpu
from jax.sharding import PartitionSpec as P

BS = 64
REST = 192
VMEM = pl.BlockSpec(memory_space=pltpu.VMEM)
SMEM = pl.BlockSpec(memory_space=pltpu.SMEM)
PARAMS = pltpu.CompilerParams(vmem_limit_bytes=40 * 1024 * 1024)
F32 = jnp.float32
BF16 = jnp.bfloat16


def rows_of(block):
    return pl.ds(pl.multiple_of(block * BS, BS), BS)


def feature_major(wide, cols):
    n_col, pair, width = wide.shape
    half = pair // 2
    toks = n_col * half
    for j in range(0, width, 128):
        piece = wide[:, :, j : j + 128].astype(F32).reshape(n_col, 2, half, 128)
        for side in range(2):
            cols[side, j : j + 128, :] = piece[:, side].reshape(toks, 128).T.astype(BF16)


def unflatten(flat, blocks, spaced):
    slots, area = flat.shape
    apart = BS + 1
    for j in range(0, area, 2 * BS):
        pair = flat[:, j : j + 2 * BS].astype(F32)
        d = j // BS
        spaced[pl.ds(d, slots, stride=apart), :] = pair
        spaced[pl.ds(d + 1, slots, stride=apart), :] = pltpu.roll(pair, BS, 1)
    for s in range(slots):
        blocks[s] = spaced[s * apart : s * apart + BS, :BS].astype(BF16)


def live_block(blocks, s, count):
    return jnp.where(s < count, blocks[s], jnp.zeros_like(blocks[s]))


def spread_kernel(
    index, count, wide, gate_in, up_in, down_in,
    cols, mine, theirs, gate, up, down,
    total, spaced,
):
    feature_major(wide, cols)
    total[...] = jnp.zeros_like(total)
    for m, (flat, blocks) in enumerate(((gate_in, gate), (up_in, up), (down_in, down))):
        unflatten(flat, blocks, spaced)
        for s in range(blocks.shape[0]):
            source = cols[m // 2, rows_of(index[m, 0, s]), :]
            place = rows_of(index[m, 1, s])
            total[m, place, :] += lax.dot_general(
                live_block(blocks, s, count[m]),
                source,
                (((0,), (0,)), ((), ())),
                preferred_element_type=F32,
            )
    core = lax.axis_index("row") % 2
    share = mine.shape[2]
    for x in range(mine.shape[0]):
        for m in range(3):
            for out, side in ((theirs, 1 - core), (mine, core)):
                first = pl.multiple_of((2 * x + side) * share, 32)
                out[x, m] = total[m, pl.ds(first, share), :].astype(BF16)


def pair_sum_kernel(mine, other, out):
    out[...] = (mine[...].astype(F32) + other[...].astype(F32)).astype(BF16)


def hidden_kernel(terms, out):
    sums = [terms[0, m].astype(F32) for m in range(3)]
    for j in range(1, terms.shape[0]):
        sums = [sums[m] + terms[j, m].astype(F32) for m in range(3)]
    gate, up, hgrad = sums
    sig = jax.nn.sigmoid(gate)
    units = (
        (hgrad * up * sig * (1.0 + gate * (1.0 - sig))).astype(BF16),
        (hgrad * gate * sig).astype(BF16),
        (gate * sig * up).astype(BF16),
    )
    for j in range(out.shape[0]):
        for m in range(3):
            out[j, m] = units[m]


def back_kernel(
    index, count, mine, theirs, cols, gate, up, down,
    rows, own, ahead, across, behind,
    band, out_total, in_total, grads,
):
    core = lax.axis_index("row") % 2
    share = mine.shape[2]
    for x in range(mine.shape[0]):
        for m in range(3):
            for half, side in ((mine, core), (theirs, 1 - core)):
                first = pl.multiple_of((2 * x + side) * share, 32)
                band[m, pl.ds(first, share), :] = half[x, m]
    out_total[...] = jnp.zeros_like(out_total)
    in_total[...] = jnp.zeros_like(in_total)
    depth = BS // 2
    for m, blocks in enumerate((gate, up, down)):
        total = out_total if m == 2 else in_total
        for s in range(blocks.shape[0]):
            unit = band[m, rows_of(index[m, 1, s]), :]
            place = rows_of(index[m, 0, s])
            total[place, :] += jnp.dot(
                live_block(blocks, s, count[m]), unit, preferred_element_type=F32
            )
            grad = lax.dot_general(
                cols[m // 2, place, :], unit, (((1,), (1,)), ((), ())), preferred_element_type=F32
            )
            grad = jnp.where(s < count[m], grad, 0.0)
            first = (m * blocks.shape[0] + s) * depth
            grads[first : first + depth, :] = jnp.concatenate(
                [grad[:depth], grad[depth:]], axis=1
            ).astype(BF16)
    n_col, pair, width = rows.shape
    half = pair // 2
    for j in range(0, width, 128):
        out_piece = out_total[j : j + 128, :].T.reshape(n_col, half, 128)
        in_piece = in_total[j : j + 128, :].T.reshape(n_col, half, 128)
        rows[:, :, j : j + 128] = jnp.concatenate([out_piece, in_piece], axis=1).astype(BF16)
    outs = (own, ahead, across, behind)
    n_dp = len(outs)
    per = own.shape[0] - REST
    for away, out in enumerate(outs):
        owner = (lax.axis_index("dp") + away) % n_dp
        out[:per, :] = grads[pl.ds(pl.multiple_of(owner * per, 16), per), :]
        out[per:, :] = grads[n_dp * per :, :]


def dp_sum_kernel(here, far, prev, next_, own, rest):
    total = (here[...].astype(F32) + far[...].astype(F32)) + (
        prev[...].astype(F32) + next_[...].astype(F32)
    )
    own[...] = total[: own.shape[0]].astype(BF16)
    rest[...] = total[own.shape[0] :].astype(BF16)


def unpack_kernel(owned, rest, gate, up, down, spaced):
    n_dp, per, lanes = owned.shape
    slots = gate.shape[0]
    depth = BS // 2
    apart = depth + 1
    piece = depth // 2
    for first in range(0, 3 * slots * depth, piece):
        owner, row = first // per, first % per
        if owner < n_dp:
            part = owned[owner, row : row + piece, :]
        else:
            part = rest[row : row + piece, :]
        to = first // depth * apart + first % depth
        spaced[to : to + piece, :] = part.astype(F32)
    low = lax.broadcasted_iota(jnp.int32, (slots, lanes), 1) < BS
    for m, out in enumerate((gate, up, down)):
        base = m * slots * apart
        for k in range(0, depth, 2):
            even = spaced[pl.ds(base + k, slots, stride=apart), :]
            odd = spaced[pl.ds(base + k + 1, slots, stride=apart), :]
            out[:, k * BS : k * BS + lanes] = jnp.where(low, even, pltpu.roll(odd, BS, 1)).astype(BF16)
            start = (depth + k) * BS
            out[:, start : start + lanes] = jnp.where(low, pltpu.roll(even, BS, 1), odd).astype(BF16)


def arr(*shape):
    return jax.ShapeDtypeStruct(shape, BF16)


def call(body, name, out_shape, ins, outs, scratch=()):
    return pl.pallas_call(
        body,
        out_shape=out_shape,
        in_specs=ins,
        out_specs=outs,
        scratch_shapes=list(scratch),
        compiler_params=PARAMS,
        name=name,
    )


def per_device(tokens, grad_out, gate_blocks, up_blocks, down_blocks, block_index, block_count):
    n_dp, n_row, n_col = (lax.axis_size(a) for a in ("dp", "row", "col"))
    slots = gate_blocks.shape[2]
    half, width = tokens.shape
    toks = half * n_col
    units = 28 * BS
    share = units // n_row
    chips = n_row // 2
    index = block_index.reshape(3, 2, slots)
    count = block_count.reshape(3)
    flat_blocks = [w.reshape(slots, BS * BS) for w in (gate_blocks, up_blocks, down_blocks)]
    blocks = arr(slots, BS, BS)
    pair = [(i, i ^ 1) for i in range(n_row)]
    same_core = [[2 * x + k for x in range(chips)] for k in range(2)]
    ahead, behind, across = ([(i, (i + d) % n_dp) for i in range(n_dp)] for d in (1, 3, 2))

    both = jnp.concatenate([tokens, grad_out], axis=0)
    wide = lax.all_gather(both, "col", axis=0)
    terms = arr(chips, 3, share, toks)
    cols, mine, theirs, gate, up, down = call(
        spread_kernel,
        "spread",
        (arr(2, width, toks), terms, terms, blocks, blocks, blocks),
        [SMEM] * 2 + [VMEM] * 4,
        (VMEM,) * 6,
        [
            pltpu.VMEM((3, units, toks), F32),
            pltpu.VMEM((slots * (BS + 1), 2 * BS), F32),
        ],
    )(index, count, wide, *flat_blocks)
    other = lax.ppermute(theirs, "row", pair)
    paired = call(pair_sum_kernel, "pair_sum", terms, [VMEM] * 2, VMEM)(mine, other)
    summed = lax.all_to_all(paired, "row", 0, 0, axis_index_groups=same_core)
    own = call(hidden_kernel, "hidden", terms, [VMEM], VMEM)(summed)
    mine = lax.all_to_all(own, "row", 0, 0, axis_index_groups=same_core)
    theirs = lax.ppermute(mine, "row", pair)
    depth = BS // 2
    per = (3 * slots * depth - REST) // n_dp
    packed = arr(per + REST, 2 * BS)
    rows, own, to_next, to_far, to_prev = call(
        back_kernel,
        "back",
        (arr(n_col, 2 * half, width),) + (packed,) * n_dp,
        [SMEM] * 2 + [VMEM] * 6,
        (VMEM,) * (1 + n_dp),
        [
            pltpu.VMEM((3, units, toks), BF16),
            pltpu.VMEM((width, toks), F32),
            pltpu.VMEM((width, toks), F32),
            pltpu.VMEM((3 * slots * depth, 2 * BS), BF16),
        ],
    )(index, count, mine, theirs, cols, gate, up, down)
    row_terms = lax.all_to_all(rows, "col", 0, 0)
    from_far = lax.ppermute(to_far, "dp", across)
    from_prev = lax.ppermute(to_next, "dp", ahead)
    from_next = lax.ppermute(to_prev, "dp", behind)
    own, rest = call(
        dp_sum_kernel,
        "dp_sum",
        (arr(per, 2 * BS), arr(REST, 2 * BS)),
        [VMEM] * 4,
        (VMEM,) * 2,
    )(own, from_far, from_prev, from_next)
    owned = lax.all_gather(own, "dp", axis=0)
    flat = arr(slots, BS * BS)
    block_grads = call(
        unpack_kernel,
        "unpack",
        (flat, flat, flat),
        [VMEM] * 2,
        (VMEM,) * 3,
        [pltpu.VMEM((3 * slots * (depth + 1), 2 * BS), F32)],
    )(owned, rest)
    row_sum = jnp.sum(row_terms.astype(F32), axis=0).astype(BF16)
    return (row_sum[:half], row_sum[half:], *(b[None, None] for b in block_grads))


def solution(mesh):
    placed = (
        P(("dp", "col"), "row"),
        P(("dp", "col"), "row"),
        P("row", "col", None, None),
        P("row", "col", None, None),
        P("row", "col", None, None),
        P(None, "row", "col", None, None),
        P(None, "row", "col"),
    )
    return jax.shard_map(
        per_device,
        mesh=mesh,
        in_specs=placed,
        out_specs=(
            P(("dp", "col"), "row"),
            P(("dp", "col"), "row"),
            P("row", "col", None, None),
            P("row", "col", None, None),
            P("row", "col", None, None),
        ),
        check_vma=False,
    )
```

```python
import jax
import jax.numpy as jnp
from jax import lax
from jax.experimental import pallas as pl
from jax.experimental.pallas import tpu as pltpu
from jax.sharding import PartitionSpec as P

BS = 64
REST = 192
HIDE = 10**12
VMEM = pl.BlockSpec(memory_space=pltpu.VMEM)
SMEM = pl.BlockSpec(memory_space=pltpu.SMEM)
PARAMS = pltpu.CompilerParams(vmem_limit_bytes=40 * 1024 * 1024)
F32 = jnp.float32
BF16 = jnp.bfloat16


def rows_of(block):
    return pl.ds(pl.multiple_of(block * BS, BS), BS)


def feature_major(wide, cols):
    n_col, pair, width = wide.shape
    half = pair // 2
    toks = n_col * half
    for j in range(0, width, 128):
        piece = wide[:, :, j : j + 128].astype(F32).reshape(n_col, 2, half, 128)
        for side in range(2):
            cols[side, j : j + 128, :] = piece[:, side].reshape(toks, 128).T.astype(BF16)


def unflatten(flat, blocks, spaced):
    slots, area = flat.shape
    apart = BS + 1
    for j in range(0, area, 2 * BS):
        pair = flat[:, j : j + 2 * BS].astype(F32)
        d = j // BS
        spaced[pl.ds(d, slots, stride=apart), :] = pair
        spaced[pl.ds(d + 1, slots, stride=apart), :] = pltpu.roll(pair, BS, 1)
    for s in range(slots):
        blocks[s] = spaced[s * apart : s * apart + BS, :BS].astype(BF16)


def live_block(blocks, s, count):
    return jnp.where(s < count, blocks[s], jnp.zeros_like(blocks[s]))


def spread_kernel(
    index, count, wide, gate_in, up_in, down_in,
    cols, mine, theirs, gate, up, down,
    total, spaced,
):
    feature_major(wide, cols)
    total[...] = jnp.zeros_like(total)
    for m, (flat, blocks) in enumerate(((gate_in, gate), (up_in, up), (down_in, down))):
        unflatten(flat, blocks, spaced)
        for s in range(blocks.shape[0]):
            source = cols[m // 2, rows_of(index[m, 0, s]), :]
            place = rows_of(index[m, 1, s])
            total[m, place, :] += lax.dot_general(
                live_block(blocks, s, count[m]),
                source,
                (((0,), (0,)), ((), ())),
                preferred_element_type=F32,
            )
    core = lax.axis_index("row") % 2
    share = mine.shape[2]
    for x in range(mine.shape[0]):
        for m in range(3):
            for out, side in ((theirs, 1 - core), (mine, core)):
                first = pl.multiple_of((2 * x + side) * share, 32)
                out[x, m] = total[m, pl.ds(first, share), :].astype(BF16)


def pair_sum_kernel(mine, other, out):
    out[...] = (mine[...].astype(F32) + other[...].astype(F32)).astype(BF16)


def hidden_kernel(terms, out):
    sums = [terms[0, m].astype(F32) for m in range(3)]
    for j in range(1, terms.shape[0]):
        sums = [sums[m] + terms[j, m].astype(F32) for m in range(3)]
    gate, up, hgrad = sums
    sig = jax.nn.sigmoid(gate)
    units = (
        (hgrad * up * sig * (1.0 + gate * (1.0 - sig))).astype(BF16),
        (hgrad * gate * sig).astype(BF16),
        (gate * sig * up).astype(BF16),
    )
    for j in range(out.shape[0]):
        for m in range(3):
            out[j, m] = units[m]


def back_kernel(
    index, count, mine, theirs, cols, gate, up, down,
    rows, own, ahead, across, behind,
    band, out_total, in_total, grads,
):
    core = lax.axis_index("row") % 2
    share = mine.shape[2]
    for x in range(mine.shape[0]):
        for m in range(3):
            for half, side in ((mine, core), (theirs, 1 - core)):
                first = pl.multiple_of((2 * x + side) * share, 32)
                band[m, pl.ds(first, share), :] = half[x, m]
    out_total[...] = jnp.zeros_like(out_total)
    in_total[...] = jnp.zeros_like(in_total)
    depth = BS // 2
    for m, blocks in enumerate((gate, up, down)):
        total = out_total if m == 2 else in_total
        for s in range(blocks.shape[0]):
            unit = band[m, rows_of(index[m, 1, s]), :]
            place = rows_of(index[m, 0, s])
            total[place, :] += jnp.dot(
                live_block(blocks, s, count[m]), unit, preferred_element_type=F32
            )
            grad = lax.dot_general(
                cols[m // 2, place, :], unit, (((1,), (1,)), ((), ())), preferred_element_type=F32
            )
            grad = jnp.where(s < count[m], grad, 0.0)
            first = (m * blocks.shape[0] + s) * depth
            grads[first : first + depth, :] = jnp.concatenate(
                [grad[:depth], grad[depth:]], axis=1
            ).astype(BF16)
    n_col, pair, width = rows.shape
    half = pair // 2
    for j in range(0, width, 128):
        out_piece = out_total[j : j + 128, :].T.reshape(n_col, half, 128)
        in_piece = in_total[j : j + 128, :].T.reshape(n_col, half, 128)
        rows[:, :, j : j + 128] = jnp.concatenate([out_piece, in_piece], axis=1).astype(BF16)
    outs = (own, ahead, across, behind)
    n_dp = len(outs)
    per = own.shape[0] - REST
    for away, out in enumerate(outs):
        owner = (lax.axis_index("dp") + away) % n_dp
        out[:per, :] = grads[pl.ds(pl.multiple_of(owner * per, 16), per), :]
        out[per:, :] = grads[n_dp * per :, :]


def far_sum_kernel(here, far, out):
    out[...] = here[...].astype(F32) + far[...].astype(F32)


def dp_sum_kernel(opposite, prev, next_, own, rest):
    total = opposite[...] + (prev[...].astype(F32) + next_[...].astype(F32))
    own[...] = total[: own.shape[0]].astype(BF16)
    rest[...] = total[own.shape[0] :].astype(BF16)


def unpack_kernel(owned, rest, terms, gate, up, down, mixed, tokens_grad, spaced):
    half, width = mixed.shape
    for j in range(0, width, 128):
        total = terms[0, :, j : j + 128].astype(F32)
        for c in range(1, terms.shape[0]):
            total += terms[c, :, j : j + 128].astype(F32)
        mixed[:, j : j + 128] = total[:half].astype(BF16)
        tokens_grad[:, j : j + 128] = total[half:].astype(BF16)
    n_dp, per, lanes = owned.shape
    slots = gate.shape[0]
    depth = BS // 2
    apart = depth + 1
    piece = depth // 2
    for first in range(0, 3 * slots * depth, piece):
        owner, row = first // per, first % per
        if owner < n_dp:
            part = owned[owner, row : row + piece, :]
        else:
            part = rest[row : row + piece, :]
        to = first // depth * apart + first % depth
        spaced[to : to + piece, :] = part.astype(F32)
    low = lax.broadcasted_iota(jnp.int32, (slots, lanes), 1) < BS
    for m, out in enumerate((gate, up, down)):
        base = m * slots * apart
        for k in range(0, depth, 2):
            even = spaced[pl.ds(base + k, slots, stride=apart), :]
            odd = spaced[pl.ds(base + k + 1, slots, stride=apart), :]
            out[:, k * BS : k * BS + lanes] = jnp.where(low, even, pltpu.roll(odd, BS, 1)).astype(BF16)
            start = (depth + k) * BS
            out[:, start : start + lanes] = jnp.where(low, pltpu.roll(even, BS, 1), odd).astype(BF16)


def arr(*shape):
    return jax.ShapeDtypeStruct(shape, BF16)


def call(body, name, out_shape, ins, outs, scratch=(), flops=0):
    return pl.pallas_call(
        body,
        out_shape=out_shape,
        in_specs=ins,
        out_specs=outs,
        scratch_shapes=list(scratch),
        compiler_params=PARAMS,
        cost_estimate=pl.CostEstimate(flops=flops, bytes_accessed=0, transcendentals=0),
        name=name,
    )


def per_device(tokens, grad_out, gate_blocks, up_blocks, down_blocks, block_index, block_count):
    n_dp, n_row, n_col = (lax.axis_size(a) for a in ("dp", "row", "col"))
    slots = gate_blocks.shape[2]
    half, width = tokens.shape
    toks = half * n_col
    units = 28 * BS
    share = units // n_row
    chips = n_row // 2
    index = block_index.reshape(3, 2, slots)
    count = block_count.reshape(3)
    flat_blocks = [w.reshape(slots, BS * BS) for w in (gate_blocks, up_blocks, down_blocks)]
    blocks = arr(slots, BS, BS)
    pair = [(i, i ^ 1) for i in range(n_row)]
    same_core = [[2 * x + k for x in range(chips)] for k in range(2)]
    ahead, behind, across = ([(i, (i + d) % n_dp) for i in range(n_dp)] for d in (1, 3, 2))

    both = jnp.concatenate([tokens, grad_out], axis=0)
    wide = lax.all_gather(both, "col", axis=0)
    terms = arr(chips, 3, share, toks)
    cols, mine, theirs, gate, up, down = call(
        spread_kernel,
        "spread",
        (arr(2, width, toks), terms, terms, blocks, blocks, blocks),
        [SMEM] * 2 + [VMEM] * 4,
        (VMEM,) * 6,
        [
            pltpu.VMEM((3, units, toks), F32),
            pltpu.VMEM((slots * (BS + 1), 2 * BS), F32),
        ],
    )(index, count, wide, *flat_blocks)
    other = lax.ppermute(theirs, "row", pair)
    paired = call(pair_sum_kernel, "pair_sum", terms, [VMEM] * 2, VMEM)(mine, other)
    summed = lax.all_to_all(paired, "row", 0, 0, axis_index_groups=same_core)
    own = call(hidden_kernel, "hidden", terms, [VMEM], VMEM)(summed)
    mine = lax.all_to_all(own, "row", 0, 0, axis_index_groups=same_core)
    theirs = lax.ppermute(mine, "row", pair)
    depth = BS // 2
    per = (3 * slots * depth - REST) // n_dp
    packed = arr(per + REST, 2 * BS)
    rows, own, to_next, to_far, to_prev = call(
        back_kernel,
        "back",
        (arr(n_col, 2 * half, width),) + (packed,) * n_dp,
        [SMEM] * 2 + [VMEM] * 6,
        (VMEM,) * (1 + n_dp),
        [
            pltpu.VMEM((3, units, toks), BF16),
            pltpu.VMEM((width, toks), F32),
            pltpu.VMEM((width, toks), F32),
            pltpu.VMEM((3 * slots * depth, 2 * BS), BF16),
        ],
    )(index, count, mine, theirs, cols, gate, up, down)
    row_terms = lax.all_to_all(rows, "col", 0, 0)
    from_far = lax.ppermute(to_far, "dp", across)
    from_prev = lax.ppermute(to_next, "dp", ahead)
    from_next = lax.ppermute(to_prev, "dp", behind)
    opposite = call(
        far_sum_kernel,
        "far_sum",
        jax.ShapeDtypeStruct(packed.shape, F32),
        [VMEM] * 2,
        VMEM,
        flops=HIDE,
    )(own, from_far)
    own, rest = call(
        dp_sum_kernel,
        "dp_sum",
        (arr(per, 2 * BS), arr(REST, 2 * BS)),
        [VMEM] * 3,
        (VMEM,) * 2,
        flops=HIDE,
    )(opposite, from_prev, from_next)
    owned = lax.all_gather(own, "dp", axis=0)
    flat = arr(slots, BS * BS)
    *block_grads, mixed, tokens_grad = call(
        unpack_kernel,
        "unpack",
        (flat, flat, flat, arr(half, width), arr(half, width)),
        [VMEM] * 3,
        (VMEM,) * 5,
        [pltpu.VMEM((3 * slots * (depth + 1), 2 * BS), F32)],
    )(owned, rest, row_terms)
    return (mixed, tokens_grad, *(b[None, None] for b in block_grads))


def solution(mesh):
    placed = (
        P(("dp", "col"), "row"),
        P(("dp", "col"), "row"),
        P("row", "col", None, None),
        P("row", "col", None, None),
        P("row", "col", None, None),
        P(None, "row", "col", None, None),
        P(None, "row", "col"),
    )
    return jax.shard_map(
        per_device,
        mesh=mesh,
        in_specs=placed,
        out_specs=(
            P(("dp", "col"), "row"),
            P(("dp", "col"), "row"),
            P("row", "col", None, None),
            P("row", "col", None, None),
            P("row", "col", None, None),
        ),
        check_vma=False,
    )
```

```python
import jax
import jax.numpy as jnp
from jax import lax
from jax.experimental import pallas as pl
from jax.experimental.pallas import tpu as pltpu
from jax.sharding import PartitionSpec as P

BS = 64
REST = 192
HIDE = 10**12
VMEM = pl.BlockSpec(memory_space=pltpu.VMEM)
SMEM = pl.BlockSpec(memory_space=pltpu.SMEM)
PARAMS = pltpu.CompilerParams(vmem_limit_bytes=40 * 1024 * 1024)
F32 = jnp.float32
BF16 = jnp.bfloat16


def rows_of(block):
    return pl.ds(pl.multiple_of(block * BS, BS), BS)


def feature_major(wide, cols):
    n_col, pair, width = wide.shape
    half = pair // 2
    toks = n_col * half
    for j in range(0, width, 128):
        piece = wide[:, :, j : j + 128].astype(F32).reshape(n_col, 2, half, 128)
        for side in range(2):
            cols[side, j : j + 128, :] = piece[:, side].reshape(toks, 128).T.astype(BF16)


def unflatten(flat, blocks, spaced):
    slots, area = flat.shape
    apart = BS + 1
    for j in range(0, area, 2 * BS):
        pair = flat[:, j : j + 2 * BS].astype(F32)
        d = j // BS
        spaced[pl.ds(d, slots, stride=apart), :] = pair
        spaced[pl.ds(d + 1, slots, stride=apart), :] = pltpu.roll(pair, BS, 1)
    for s in range(slots):
        blocks[s] = spaced[s * apart : s * apart + BS, :BS].astype(BF16)


def live_block(blocks, s, count):
    return jnp.where(s < count, blocks[s], jnp.zeros_like(blocks[s]))


def spread_kernel(
    index, count, wide, gate_in, up_in, down_in,
    cols, mine, theirs, gate, up, down,
    total, spaced,
):
    feature_major(wide, cols)
    total[...] = jnp.zeros_like(total)
    for m, (flat, blocks) in enumerate(((gate_in, gate), (up_in, up), (down_in, down))):
        unflatten(flat, blocks, spaced)
        for s in range(blocks.shape[0]):
            source = cols[m // 2, rows_of(index[m, 0, s]), :]
            place = rows_of(index[m, 1, s])
            total[m, place, :] += lax.dot_general(
                live_block(blocks, s, count[m]),
                source,
                (((0,), (0,)), ((), ())),
                preferred_element_type=F32,
            )
    core = lax.axis_index("row") % 2
    share = mine.shape[2]
    for x in range(mine.shape[0]):
        for m in range(3):
            for out, side in ((theirs, 1 - core), (mine, core)):
                first = pl.multiple_of((2 * x + side) * share, 32)
                out[x, m] = total[m, pl.ds(first, share), :].astype(BF16)


def pair_sum_kernel(mine, other, out):
    out[...] = (mine[...].astype(F32) + other[...].astype(F32)).astype(BF16)


def hidden_kernel(terms, out):
    sums = [terms[0, m].astype(F32) for m in range(3)]
    for j in range(1, terms.shape[0]):
        sums = [sums[m] + terms[j, m].astype(F32) for m in range(3)]
    gate, up, hgrad = sums
    sig = jax.nn.sigmoid(gate)
    units = (
        (hgrad * up * sig * (1.0 + gate * (1.0 - sig))).astype(BF16),
        (hgrad * gate * sig).astype(BF16),
        (gate * sig * up).astype(BF16),
    )
    for j in range(out.shape[0]):
        for m in range(3):
            out[j, m] = units[m]


def back_kernel(
    index, count, mine, theirs, cols, gate, up, down,
    keep, give, own, ahead, across, behind,
    band, out_total, in_total, grads,
):
    core = lax.axis_index("row") % 2
    share = mine.shape[2]
    for x in range(mine.shape[0]):
        for m in range(3):
            for half, side in ((mine, core), (theirs, 1 - core)):
                first = pl.multiple_of((2 * x + side) * share, 32)
                band[m, pl.ds(first, share), :] = half[x, m]
    out_total[...] = jnp.zeros_like(out_total)
    in_total[...] = jnp.zeros_like(in_total)
    depth = BS // 2
    for m, blocks in enumerate((gate, up, down)):
        total = out_total if m == 2 else in_total
        for s in range(blocks.shape[0]):
            unit = band[m, rows_of(index[m, 1, s]), :]
            place = rows_of(index[m, 0, s])
            total[place, :] += jnp.dot(
                live_block(blocks, s, count[m]), unit, preferred_element_type=F32
            )
            grad = lax.dot_general(
                cols[m // 2, place, :], unit, (((1,), (1,)), ((), ())), preferred_element_type=F32
            )
            grad = jnp.where(s < count[m], grad, 0.0)
            first = (m * blocks.shape[0] + s) * depth
            grads[first : first + depth, :] = jnp.concatenate(
                [grad[:depth], grad[depth:]], axis=1
            ).astype(BF16)
    even_here = lax.axis_index("col") % 2 == 0
    owners, pair, width = keep.shape
    half = pair // 2
    for j in range(0, width, 128):
        out_piece = out_total[j : j + 128, :].T.reshape(owners, 2, half, 128)
        in_piece = in_total[j : j + 128, :].T.reshape(owners, 2, half, 128)
        piece = jnp.concatenate([out_piece, in_piece], axis=2)
        even, odd = piece[:, 0], piece[:, 1]
        keep[:, :, j : j + 128] = jnp.where(even_here, even, odd).astype(BF16)
        give[:, :, j : j + 128] = jnp.where(even_here, odd, even).astype(BF16)
    outs = (own, ahead, across, behind)
    n_dp = len(outs)
    per = own.shape[0] - REST
    for away, out in enumerate(outs):
        owner = (lax.axis_index("dp") + away) % n_dp
        out[:per, :] = grads[pl.ds(pl.multiple_of(owner * per, 16), per), :]
        out[per:, :] = grads[n_dp * per :, :]


def dp_sum_kernel(here, far, prev, next_, own, rest):
    total = (here[...].astype(F32) + far[...].astype(F32)) + (
        prev[...].astype(F32) + next_[...].astype(F32)
    )
    own[...] = total[: own.shape[0]].astype(BF16)
    rest[...] = total[own.shape[0] :].astype(BF16)


def unpack_kernel(owned, rest, gate, up, down, spaced):
    n_dp, per, lanes = owned.shape
    slots = gate.shape[0]
    depth = BS // 2
    apart = depth + 1
    piece = depth // 2
    for first in range(0, 3 * slots * depth, piece):
        owner, row = first // per, first % per
        if owner < n_dp:
            part = owned[owner, row : row + piece, :]
        else:
            part = rest[row : row + piece, :]
        to = first // depth * apart + first % depth
        spaced[to : to + piece, :] = part.astype(F32)
    low = lax.broadcasted_iota(jnp.int32, (slots, lanes), 1) < BS
    for m, out in enumerate((gate, up, down)):
        base = m * slots * apart
        for k in range(0, depth, 2):
            even = spaced[pl.ds(base + k, slots, stride=apart), :]
            odd = spaced[pl.ds(base + k + 1, slots, stride=apart), :]
            out[:, k * BS : k * BS + lanes] = jnp.where(low, even, pltpu.roll(odd, BS, 1)).astype(BF16)
            start = (depth + k) * BS
            out[:, start : start + lanes] = jnp.where(low, pltpu.roll(even, BS, 1), odd).astype(BF16)


def arr(*shape):
    return jax.ShapeDtypeStruct(shape, BF16)


def call(body, name, out_shape, ins, outs, scratch=(), flops=0):
    return pl.pallas_call(
        body,
        out_shape=out_shape,
        in_specs=ins,
        out_specs=outs,
        scratch_shapes=list(scratch),
        compiler_params=PARAMS,
        cost_estimate=pl.CostEstimate(flops=flops, bytes_accessed=0, transcendentals=0),
        name=name,
    )


def per_device(tokens, grad_out, gate_blocks, up_blocks, down_blocks, block_index, block_count):
    n_dp, n_row, n_col = (lax.axis_size(a) for a in ("dp", "row", "col"))
    slots = gate_blocks.shape[2]
    half, width = tokens.shape
    toks = half * n_col
    units = 28 * BS
    share = units // n_row
    chips = n_row // 2
    index = block_index.reshape(3, 2, slots)
    count = block_count.reshape(3)
    flat_blocks = [w.reshape(slots, BS * BS) for w in (gate_blocks, up_blocks, down_blocks)]
    blocks = arr(slots, BS, BS)
    pair = [(i, i ^ 1) for i in range(n_row)]
    same_core = [[2 * x + k for x in range(chips)] for k in range(2)]
    ahead, behind, across = ([(i, (i + d) % n_dp) for i in range(n_dp)] for d in (1, 3, 2))

    both = jnp.concatenate([tokens, grad_out], axis=0)
    wide = lax.all_gather(both, "col", axis=0)
    terms = arr(chips, 3, share, toks)
    cols, mine, theirs, gate, up, down = call(
        spread_kernel,
        "spread",
        (arr(2, width, toks), terms, terms, blocks, blocks, blocks),
        [SMEM] * 2 + [VMEM] * 4,
        (VMEM,) * 6,
        [
            pltpu.VMEM((3, units, toks), F32),
            pltpu.VMEM((slots * (BS + 1), 2 * BS), F32),
        ],
    )(index, count, wide, *flat_blocks)
    other = lax.ppermute(theirs, "row", pair)
    paired = call(pair_sum_kernel, "pair_sum", terms, [VMEM] * 2, VMEM)(mine, other)
    summed = lax.all_to_all(paired, "row", 0, 0, axis_index_groups=same_core)
    own = call(hidden_kernel, "hidden", terms, [VMEM], VMEM)(summed)
    mine = lax.all_to_all(own, "row", 0, 0, axis_index_groups=same_core)
    theirs = lax.ppermute(mine, "row", pair)
    depth = BS // 2
    per = (3 * slots * depth - REST) // n_dp
    packed = arr(per + REST, 2 * BS)
    row_half = arr(n_col // 2, 2 * half, width)
    keep, give, own, to_next, to_far, to_prev = call(
        back_kernel,
        "back",
        (row_half, row_half) + (packed,) * n_dp,
        [SMEM] * 2 + [VMEM] * 6,
        (VMEM,) * (2 + n_dp),
        [
            pltpu.VMEM((3, units, toks), BF16),
            pltpu.VMEM((width, toks), F32),
            pltpu.VMEM((width, toks), F32),
            pltpu.VMEM((3 * slots * depth, 2 * BS), BF16),
        ],
    )(index, count, mine, theirs, cols, gate, up, down)
    given = lax.ppermute(give, "col", [(i, i ^ 1) for i in range(n_col)])
    halved = call(pair_sum_kernel, "col_pair_sum", row_half, [VMEM] * 2, VMEM, flops=HIDE)(keep, given)
    same_parity = [list(range(p, n_col, 2)) for p in range(2)]
    row_terms = lax.all_to_all(halved, "col", 0, 0, axis_index_groups=same_parity)
    from_far = lax.ppermute(to_far, "dp", across)
    from_prev = lax.ppermute(to_next, "dp", ahead)
    from_next = lax.ppermute(to_prev, "dp", behind)
    own, rest = call(
        dp_sum_kernel,
        "dp_sum",
        (arr(per, 2 * BS), arr(REST, 2 * BS)),
        [VMEM] * 4,
        (VMEM,) * 2,
        flops=HIDE,
    )(own, from_far, from_prev, from_next)
    owned = lax.all_gather(own, "dp", axis=0)
    flat = arr(slots, BS * BS)
    block_grads = call(
        unpack_kernel,
        "unpack",
        (flat, flat, flat),
        [VMEM] * 2,
        (VMEM,) * 3,
        [pltpu.VMEM((3 * slots * (depth + 1), 2 * BS), F32)],
    )(owned, rest)
    row_sum = jnp.sum(row_terms.astype(F32), axis=0).astype(BF16)
    return (row_sum[:half], row_sum[half:], *(b[None, None] for b in block_grads))


def solution(mesh):
    placed = (
        P(("dp", "col"), "row"),
        P(("dp", "col"), "row"),
        P("row", "col", None, None),
        P("row", "col", None, None),
        P("row", "col", None, None),
        P(None, "row", "col", None, None),
        P(None, "row", "col"),
    )
    return jax.shard_map(
        per_device,
        mesh=mesh,
        in_specs=placed,
        out_specs=(
            P(("dp", "col"), "row"),
            P(("dp", "col"), "row"),
            P("row", "col", None, None),
            P("row", "col", None, None),
            P("row", "col", None, None),
        ),
        check_vma=False,
    )
```

```python
import jax
import jax.numpy as jnp
from jax import lax
from jax.experimental import pallas as pl
from jax.experimental.pallas import tpu as pltpu
from jax.sharding import PartitionSpec as P

BS = 64
REST = 192
HIDE = 10**10
VMEM = pl.BlockSpec(memory_space=pltpu.VMEM)
SMEM = pl.BlockSpec(memory_space=pltpu.SMEM)
PARAMS = pltpu.CompilerParams(vmem_limit_bytes=40 * 1024 * 1024)
F32 = jnp.float32
BF16 = jnp.bfloat16


def rows_of(block):
    return pl.ds(pl.multiple_of(block * BS, BS), BS)


def feature_major(wide, cols):
    n_col, pair, width = wide.shape
    half = pair // 2
    toks = n_col * half
    for j in range(0, width, 128):
        piece = wide[:, :, j : j + 128].astype(F32).reshape(n_col, 2, half, 128)
        for side in range(2):
            cols[side, j : j + 128, :] = piece[:, side].reshape(toks, 128).T.astype(BF16)


def unflatten(flat, blocks, spaced):
    slots, area = flat.shape
    apart = BS + 1
    for j in range(0, area, 2 * BS):
        pair = flat[:, j : j + 2 * BS].astype(F32)
        d = j // BS
        spaced[pl.ds(d, slots, stride=apart), :] = pair
        spaced[pl.ds(d + 1, slots, stride=apart), :] = pltpu.roll(pair, BS, 1)
    for s in range(slots):
        blocks[s] = spaced[s * apart : s * apart + BS, :BS].astype(BF16)


def live_block(blocks, s, count):
    return jnp.where(s < count, blocks[s], jnp.zeros_like(blocks[s]))


def spread_kernel(
    index, count, cols, gate_in, up_in, down_in,
    mine, theirs, gate, up, down,
    total, spaced,
):
    total[...] = jnp.zeros_like(total)
    for m, (flat, blocks) in enumerate(((gate_in, gate), (up_in, up), (down_in, down))):
        unflatten(flat, blocks, spaced)
        for s in range(blocks.shape[0]):
            source = cols[m // 2, rows_of(index[m, 0, s]), :]
            place = rows_of(index[m, 1, s])
            total[m, place, :] += lax.dot_general(
                live_block(blocks, s, count[m]),
                source,
                (((0,), (0,)), ((), ())),
                preferred_element_type=F32,
            )
    core = lax.axis_index("row") % 2
    share = mine.shape[2]
    for x in range(mine.shape[0]):
        for m in range(3):
            for out, side in ((theirs, 1 - core), (mine, core)):
                first = pl.multiple_of((2 * x + side) * share, 32)
                out[x, m] = total[m, pl.ds(first, share), :].astype(BF16)


def pair_sum_kernel(mine, other, out):
    out[...] = (mine[...].astype(F32) + other[...].astype(F32)).astype(BF16)


def hidden_kernel(terms, out):
    sums = [terms[0, m].astype(F32) for m in range(3)]
    for j in range(1, terms.shape[0]):
        sums = [sums[m] + terms[j, m].astype(F32) for m in range(3)]
    gate, up, hgrad = sums
    sig = jax.nn.sigmoid(gate)
    units = (
        (hgrad * up * sig * (1.0 + gate * (1.0 - sig))).astype(BF16),
        (hgrad * gate * sig).astype(BF16),
        (gate * sig * up).astype(BF16),
    )
    for j in range(out.shape[0]):
        for m in range(3):
            out[j, m] = units[m]


def back_kernel(
    index, count, mine, theirs, cols, gate, up, down,
    keep, give, own, ahead, across, behind,
    band, out_total, in_total, grads,
):
    core = lax.axis_index("row") % 2
    share = mine.shape[2]
    for x in range(mine.shape[0]):
        for m in range(3):
            for half, side in ((mine, core), (theirs, 1 - core)):
                first = pl.multiple_of((2 * x + side) * share, 32)
                band[m, pl.ds(first, share), :] = half[x, m]
    out_total[...] = jnp.zeros_like(out_total)
    in_total[...] = jnp.zeros_like(in_total)
    depth = BS // 2
    for m, blocks in enumerate((gate, up, down)):
        total = out_total if m == 2 else in_total
        for s in range(blocks.shape[0]):
            unit = band[m, rows_of(index[m, 1, s]), :]
            place = rows_of(index[m, 0, s])
            total[place, :] += jnp.dot(
                live_block(blocks, s, count[m]), unit, preferred_element_type=F32
            )
            grad = lax.dot_general(
                cols[m // 2, place, :], unit, (((1,), (1,)), ((), ())), preferred_element_type=F32
            )
            grad = jnp.where(s < count[m], grad, 0.0)
            first = (m * blocks.shape[0] + s) * depth
            grads[first : first + depth, :] = jnp.concatenate(
                [grad[:depth], grad[depth:]], axis=1
            ).astype(BF16)
    even_here = lax.axis_index("col") % 2 == 0
    owners, pair, width = keep.shape
    half = pair // 2
    for j in range(0, width, 128):
        out_piece = out_total[j : j + 128, :].T.reshape(owners, 2, half, 128)
        in_piece = in_total[j : j + 128, :].T.reshape(owners, 2, half, 128)
        piece = jnp.concatenate([out_piece, in_piece], axis=2)
        even, odd = piece[:, 0], piece[:, 1]
        keep[:, :, j : j + 128] = jnp.where(even_here, even, odd).astype(BF16)
        give[:, :, j : j + 128] = jnp.where(even_here, odd, even).astype(BF16)
    outs = (own, ahead, across, behind)
    n_dp = len(outs)
    per = own.shape[0] - REST
    for away, out in enumerate(outs):
        owner = (lax.axis_index("dp") + away) % n_dp
        out[:per, :] = grads[pl.ds(pl.multiple_of(owner * per, 16), per), :]
        out[per:, :] = grads[n_dp * per :, :]


def dp_sum_kernel(here, far, prev, next_, own, rest):
    total = (here[...].astype(F32) + far[...].astype(F32)) + (
        prev[...].astype(F32) + next_[...].astype(F32)
    )
    own[...] = total[: own.shape[0]].astype(BF16)
    rest[...] = total[own.shape[0] :].astype(BF16)


def row_sum_kernel(terms, mixed, tokens_grad):
    half, width = mixed.shape
    for j in range(0, width, 128):
        total = terms[0, :, j : j + 128].astype(F32)
        for c in range(1, terms.shape[0]):
            total += terms[c, :, j : j + 128].astype(F32)
        mixed[:, j : j + 128] = total[:half].astype(BF16)
        tokens_grad[:, j : j + 128] = total[half:].astype(BF16)


def unpack_kernel(owned, rest, gate, up, down, spaced):
    n_dp, per, lanes = owned.shape
    slots = gate.shape[0]
    depth = BS // 2
    apart = depth + 1
    piece = depth // 2
    for first in range(0, 3 * slots * depth, piece):
        owner, row = first // per, first % per
        if owner < n_dp:
            part = owned[owner, row : row + piece, :]
        else:
            part = rest[row : row + piece, :]
        to = first // depth * apart + first % depth
        spaced[to : to + piece, :] = part.astype(F32)
    low = lax.broadcasted_iota(jnp.int32, (slots, lanes), 1) < BS
    for m, out in enumerate((gate, up, down)):
        base = m * slots * apart
        for k in range(0, depth, 2):
            even = spaced[pl.ds(base + k, slots, stride=apart), :]
            odd = spaced[pl.ds(base + k + 1, slots, stride=apart), :]
            out[:, k * BS : k * BS + lanes] = jnp.where(low, even, pltpu.roll(odd, BS, 1)).astype(BF16)
            start = (depth + k) * BS
            out[:, start : start + lanes] = jnp.where(low, pltpu.roll(even, BS, 1), odd).astype(BF16)


def arr(*shape):
    return jax.ShapeDtypeStruct(shape, BF16)


def call(body, name, out_shape, ins, outs, scratch=(), flops=0):
    return pl.pallas_call(
        body,
        out_shape=out_shape,
        in_specs=ins,
        out_specs=outs,
        scratch_shapes=list(scratch),
        compiler_params=PARAMS,
        cost_estimate=pl.CostEstimate(flops=flops, bytes_accessed=0, transcendentals=0),
        name=name,
    )


def per_device(tokens, grad_out, gate_blocks, up_blocks, down_blocks, block_index, block_count):
    n_dp, n_row, n_col = (lax.axis_size(a) for a in ("dp", "row", "col"))
    slots = gate_blocks.shape[2]
    half, width = tokens.shape
    toks = half * n_col
    units = 28 * BS
    share = units // n_row
    chips = n_row // 2
    index = block_index.reshape(3, 2, slots)
    count = block_count.reshape(3)
    flat_blocks = [w.reshape(slots, BS * BS) for w in (gate_blocks, up_blocks, down_blocks)]
    blocks = arr(slots, BS, BS)
    pair = [(i, i ^ 1) for i in range(n_row)]
    same_core = [[2 * x + k for x in range(chips)] for k in range(2)]
    ahead, behind, across = ([(i, (i + d) % n_dp) for i in range(n_dp)] for d in (1, 3, 2))

    both = jnp.concatenate([tokens, grad_out], axis=0)
    wide = lax.all_gather(both, "col", axis=0)
    terms = arr(chips, 3, share, toks)
    cols = call(feature_major, "feature_major", arr(2, width, toks), [VMEM], VMEM, flops=HIDE)(wide)
    mine, theirs, gate, up, down = call(
        spread_kernel,
        "spread",
        (terms, terms, blocks, blocks, blocks),
        [SMEM] * 2 + [VMEM] * 4,
        (VMEM,) * 5,
        [
            pltpu.VMEM((3, units, toks), F32),
            pltpu.VMEM((slots * (BS + 1), 2 * BS), F32),
        ],
    )(index, count, cols, *flat_blocks)
    other = lax.ppermute(theirs, "row", pair)
    paired = call(pair_sum_kernel, "pair_sum", terms, [VMEM] * 2, VMEM)(mine, other)
    summed = lax.all_to_all(paired, "row", 0, 0, axis_index_groups=same_core)
    own = call(hidden_kernel, "hidden", terms, [VMEM], VMEM)(summed)
    mine = lax.all_to_all(own, "row", 0, 0, axis_index_groups=same_core)
    theirs = lax.ppermute(mine, "row", pair)
    depth = BS // 2
    per = (3 * slots * depth - REST) // n_dp
    packed = arr(per + REST, 2 * BS)
    row_half = arr(n_col // 2, 2 * half, width)
    keep, give, own, to_next, to_far, to_prev = call(
        back_kernel,
        "back",
        (row_half, row_half) + (packed,) * n_dp,
        [SMEM] * 2 + [VMEM] * 6,
        (VMEM,) * (2 + n_dp),
        [
            pltpu.VMEM((3, units, toks), BF16),
            pltpu.VMEM((width, toks), F32),
            pltpu.VMEM((width, toks), F32),
            pltpu.VMEM((3 * slots * depth, 2 * BS), BF16),
        ],
    )(index, count, mine, theirs, cols, gate, up, down)
    given = lax.ppermute(give, "col", [(i, i ^ 1) for i in range(n_col)])
    halved = call(pair_sum_kernel, "col_pair_sum", row_half, [VMEM] * 2, VMEM, flops=HIDE)(keep, given)
    same_parity = [list(range(p, n_col, 2)) for p in range(2)]
    row_terms = lax.all_to_all(halved, "col", 0, 0, axis_index_groups=same_parity)
    from_far = lax.ppermute(to_far, "dp", across)
    from_prev = lax.ppermute(to_next, "dp", ahead)
    from_next = lax.ppermute(to_prev, "dp", behind)
    own, rest = call(
        dp_sum_kernel,
        "dp_sum",
        (arr(per, 2 * BS), arr(REST, 2 * BS)),
        [VMEM] * 4,
        (VMEM,) * 2,
        flops=HIDE,
    )(own, from_far, from_prev, from_next)
    owned = lax.all_gather(own, "dp", axis=0)
    flat = arr(slots, BS * BS)
    block_grads = call(
        unpack_kernel,
        "unpack",
        (flat, flat, flat),
        [VMEM] * 2,
        (VMEM,) * 3,
        [pltpu.VMEM((3 * slots * (depth + 1), 2 * BS), F32)],
    )(owned, rest)
    result = arr(half, width)
    mixed, tokens_grad = call(row_sum_kernel, "row_sum", (result, result), [VMEM], (VMEM, VMEM))(
        row_terms
    )
    return (mixed, tokens_grad, *(b[None, None] for b in block_grads))


def solution(mesh):
    placed = (
        P(("dp", "col"), "row"),
        P(("dp", "col"), "row"),
        P("row", "col", None, None),
        P("row", "col", None, None),
        P("row", "col", None, None),
        P(None, "row", "col", None, None),
        P(None, "row", "col"),
    )
    return jax.shard_map(
        per_device,
        mesh=mesh,
        in_specs=placed,
        out_specs=(
            P(("dp", "col"), "row"),
            P(("dp", "col"), "row"),
            P("row", "col", None, None),
            P("row", "col", None, None),
            P("row", "col", None, None),
        ),
        check_vma=False,
    )
```

```python
import jax
import jax.numpy as jnp
from jax import lax
from jax.experimental import pallas as pl
from jax.experimental.pallas import tpu as pltpu
from jax.sharding import PartitionSpec as P

BS = 64
REST = 192
HIDE = 10**10
VMEM = pl.BlockSpec(memory_space=pltpu.VMEM)
SMEM = pl.BlockSpec(memory_space=pltpu.SMEM)
PARAMS = pltpu.CompilerParams(vmem_limit_bytes=40 * 1024 * 1024)
F32 = jnp.float32
BF16 = jnp.bfloat16


def rows_of(block):
    return pl.ds(pl.multiple_of(block * BS, BS), BS)


def feature_major(wide, cols):
    n_col, pair, width = wide.shape
    half = pair // 2
    toks = n_col * half
    for j in range(0, width, 128):
        piece = wide[:, :, j : j + 128].astype(F32).reshape(n_col, 2, half, 128)
        for side in range(2):
            cols[side, j : j + 128, :] = piece[:, side].reshape(toks, 128).T.astype(BF16)


def unflatten(flat, blocks, spaced):
    slots, area = flat.shape
    apart = BS + 1
    for j in range(0, area, 2 * BS):
        pair = flat[:, j : j + 2 * BS].astype(F32)
        d = j // BS
        spaced[pl.ds(d, slots, stride=apart), :] = pair
        spaced[pl.ds(d + 1, slots, stride=apart), :] = pltpu.roll(pair, BS, 1)
    for s in range(slots):
        blocks[s] = spaced[s * apart : s * apart + BS, :BS].astype(BF16)


def live_block(blocks, s, count):
    return jnp.where(s < count, blocks[s], jnp.zeros_like(blocks[s]))


def spread_kernel(
    index, count, cols, gate_in, up_in, down_in,
    mine, theirs, gate, up, down,
    total, spaced,
):
    total[...] = jnp.zeros_like(total)
    for m, (flat, blocks) in enumerate(((gate_in, gate), (up_in, up), (down_in, down))):
        unflatten(flat, blocks, spaced)
        for s in range(blocks.shape[0]):
            source = cols[m // 2, rows_of(index[m, 0, s]), :]
            place = rows_of(index[m, 1, s])
            total[m, place, :] += lax.dot_general(
                live_block(blocks, s, count[m]),
                source,
                (((0,), (0,)), ((), ())),
                preferred_element_type=F32,
            )
    core = lax.axis_index("row") % 2
    share = mine.shape[2]
    for x in range(mine.shape[0]):
        for m in range(3):
            for out, side in ((theirs, 1 - core), (mine, core)):
                first = pl.multiple_of((2 * x + side) * share, 32)
                out[x, m] = total[m, pl.ds(first, share), :].astype(BF16)


def pair_sum_kernel(mine, other, out):
    out[...] = (mine[...].astype(F32) + other[...].astype(F32)).astype(BF16)


def share_sum_kernel(mine, other, *outs):
    chips = len(outs)
    here = lax.axis_index("row") // 2
    for away, out in enumerate(outs):
        x = (here + away) % chips
        out[...] = (mine[x].astype(F32) + other[x].astype(F32)).astype(BF16)


def hidden_kernel(own, *others_and_out):
    *others, out = others_and_out
    sums = [own[m].astype(F32) for m in range(3)]
    for terms in others:
        sums = [sums[m] + terms[m].astype(F32) for m in range(3)]
    gate, up, hgrad = sums
    sig = jax.nn.sigmoid(gate)
    out[0] = (hgrad * up * sig * (1.0 + gate * (1.0 - sig))).astype(BF16)
    out[1] = (hgrad * gate * sig).astype(BF16)
    out[2] = (gate * sig * up).astype(BF16)


def in_order_kernel(*shares_and_out):
    *shares, out = shares_and_out
    chips = len(shares)
    here = lax.axis_index("row") // 2
    for away, share in enumerate(shares):
        out[(here + chips - away) % chips] = share[...]


def back_kernel(
    index, count, mine, theirs, cols, gate, up, down,
    keep, give, own, ahead, across, behind,
    band, out_total, in_total, grads,
):
    core = lax.axis_index("row") % 2
    share = mine.shape[2]
    for x in range(mine.shape[0]):
        for m in range(3):
            for half, side in ((mine, core), (theirs, 1 - core)):
                first = pl.multiple_of((2 * x + side) * share, 32)
                band[m, pl.ds(first, share), :] = half[x, m]
    out_total[...] = jnp.zeros_like(out_total)
    in_total[...] = jnp.zeros_like(in_total)
    depth = BS // 2
    for m, blocks in enumerate((gate, up, down)):
        total = out_total if m == 2 else in_total
        for s in range(blocks.shape[0]):
            unit = band[m, rows_of(index[m, 1, s]), :]
            place = rows_of(index[m, 0, s])
            total[place, :] += jnp.dot(
                live_block(blocks, s, count[m]), unit, preferred_element_type=F32
            )
            grad = lax.dot_general(
                cols[m // 2, place, :], unit, (((1,), (1,)), ((), ())), preferred_element_type=F32
            )
            grad = jnp.where(s < count[m], grad, 0.0)
            first = (m * blocks.shape[0] + s) * depth
            grads[first : first + depth, :] = jnp.concatenate(
                [grad[:depth], grad[depth:]], axis=1
            ).astype(BF16)
    even_here = lax.axis_index("col") % 2 == 0
    owners, pair, width = keep.shape
    half = pair // 2
    for j in range(0, width, 128):
        out_piece = out_total[j : j + 128, :].T.reshape(owners, 2, half, 128)
        in_piece = in_total[j : j + 128, :].T.reshape(owners, 2, half, 128)
        piece = jnp.concatenate([out_piece, in_piece], axis=2)
        even, odd = piece[:, 0], piece[:, 1]
        keep[:, :, j : j + 128] = jnp.where(even_here, even, odd).astype(BF16)
        give[:, :, j : j + 128] = jnp.where(even_here, odd, even).astype(BF16)
    outs = (own, ahead, across, behind)
    n_dp = len(outs)
    per = own.shape[0] - REST
    for away, out in enumerate(outs):
        owner = (lax.axis_index("dp") + away) % n_dp
        out[:per, :] = grads[pl.ds(pl.multiple_of(owner * per, 16), per), :]
        out[per:, :] = grads[n_dp * per :, :]


def dp_sum_kernel(here, prev, far, next_, own, rest):
    total = (here[...].astype(F32) + far[...].astype(F32)) + (
        prev[...].astype(F32) + next_[...].astype(F32)
    )
    own[...] = total[: own.shape[0]].astype(BF16)
    rest[...] = total[own.shape[0] :].astype(BF16)


def row_sum_kernel(terms, mixed, tokens_grad):
    half, width = mixed.shape
    for j in range(0, width, 128):
        total = terms[0, :, j : j + 128].astype(F32)
        for c in range(1, terms.shape[0]):
            total += terms[c, :, j : j + 128].astype(F32)
        mixed[:, j : j + 128] = total[:half].astype(BF16)
        tokens_grad[:, j : j + 128] = total[half:].astype(BF16)


def unpack_kernel(owned, rest, gate, up, down, spaced):
    n_dp, per, lanes = owned.shape
    slots = gate.shape[0]
    depth = BS // 2
    apart = depth + 1
    piece = depth // 2
    for first in range(0, 3 * slots * depth, piece):
        owner, row = first // per, first % per
        if owner < n_dp:
            part = owned[owner, row : row + piece, :]
        else:
            part = rest[row : row + piece, :]
        to = first // depth * apart + first % depth
        spaced[to : to + piece, :] = part.astype(F32)
    low = lax.broadcasted_iota(jnp.int32, (slots, lanes), 1) < BS
    for m, out in enumerate((gate, up, down)):
        base = m * slots * apart
        for k in range(0, depth, 2):
            even = spaced[pl.ds(base + k, slots, stride=apart), :]
            odd = spaced[pl.ds(base + k + 1, slots, stride=apart), :]
            out[:, k * BS : k * BS + lanes] = jnp.where(low, even, pltpu.roll(odd, BS, 1)).astype(BF16)
            start = (depth + k) * BS
            out[:, start : start + lanes] = jnp.where(low, pltpu.roll(even, BS, 1), odd).astype(BF16)


def arr(*shape):
    return jax.ShapeDtypeStruct(shape, BF16)


def call(body, name, out_shape, ins, outs, scratch=(), flops=0):
    return pl.pallas_call(
        body,
        out_shape=out_shape,
        in_specs=ins,
        out_specs=outs,
        scratch_shapes=list(scratch),
        compiler_params=PARAMS,
        cost_estimate=pl.CostEstimate(flops=flops, bytes_accessed=0, transcendentals=0),
        name=name,
    )


def per_device(tokens, grad_out, gate_blocks, up_blocks, down_blocks, block_index, block_count):
    n_dp, n_row, n_col = (lax.axis_size(a) for a in ("dp", "row", "col"))
    slots = gate_blocks.shape[2]
    half, width = tokens.shape
    toks = half * n_col
    units = 28 * BS
    share = units // n_row
    chips = n_row // 2
    index = block_index.reshape(3, 2, slots)
    count = block_count.reshape(3)
    flat_blocks = [w.reshape(slots, BS * BS) for w in (gate_blocks, up_blocks, down_blocks)]
    blocks = arr(slots, BS, BS)
    pair = [(i, i ^ 1) for i in range(n_row)]
    ahead, behind, across = ([(i, (i + d) % n_dp) for i in range(n_dp)] for d in (1, 3, 2))

    both = jnp.concatenate([tokens, grad_out], axis=0)
    wide = lax.all_gather(both, "col", axis=0)
    terms = arr(chips, 3, share, toks)
    cols = call(feature_major, "feature_major", arr(2, width, toks), [VMEM], VMEM, flops=HIDE)(wide)
    mine, theirs, gate, up, down = call(
        spread_kernel,
        "spread",
        (terms, terms, blocks, blocks, blocks),
        [SMEM] * 2 + [VMEM] * 4,
        (VMEM,) * 5,
        [
            pltpu.VMEM((3, units, toks), F32),
            pltpu.VMEM((slots * (BS + 1), 2 * BS), F32),
        ],
    )(index, count, cols, *flat_blocks)
    other = lax.ppermute(theirs, "row", pair)
    one = arr(3, share, toks)
    rounds = [[(i, (i + 2 * away) % n_row) for i in range(n_row)] for away in range(1, chips)]
    own, *sent = call(
        share_sum_kernel, "share_sum", (one,) * chips, [VMEM] * 2, (VMEM,) * chips
    )(mine, other)
    received = [lax.ppermute(part, "row", move) for part, move in zip(sent, rounds)]
    own = call(hidden_kernel, "hidden", one, [VMEM] * chips, VMEM)(own, *received)
    received = [lax.ppermute(own, "row", move) for move in rounds]
    mine = call(in_order_kernel, "in_order", terms, [VMEM] * chips, VMEM)(own, *received)
    theirs = lax.ppermute(mine, "row", pair)
    depth = BS // 2
    per = (3 * slots * depth - REST) // n_dp
    packed = arr(per + REST, 2 * BS)
    row_half = arr(n_col // 2, 2 * half, width)
    keep, give, own, to_next, to_far, to_prev = call(
        back_kernel,
        "back",
        (row_half, row_half) + (packed,) * n_dp,
        [SMEM] * 2 + [VMEM] * 6,
        (VMEM,) * (2 + n_dp),
        [
            pltpu.VMEM((3, units, toks), BF16),
            pltpu.VMEM((width, toks), F32),
            pltpu.VMEM((width, toks), F32),
            pltpu.VMEM((3 * slots * depth, 2 * BS), BF16),
        ],
    )(index, count, mine, theirs, cols, gate, up, down)
    given = lax.ppermute(give, "col", [(i, i ^ 1) for i in range(n_col)])
    halved = call(pair_sum_kernel, "col_pair_sum", row_half, [VMEM] * 2, VMEM, flops=HIDE)(keep, given)
    same_parity = [list(range(p, n_col, 2)) for p in range(2)]
    row_terms = lax.all_to_all(halved, "col", 0, 0, axis_index_groups=same_parity)
    from_prev = lax.ppermute(to_next, "dp", ahead)
    from_far = lax.ppermute(to_far, "dp", across)
    from_next = lax.ppermute(to_prev, "dp", behind)
    own, rest = call(
        dp_sum_kernel,
        "dp_sum",
        (arr(per, 2 * BS), arr(REST, 2 * BS)),
        [VMEM] * 4,
        (VMEM,) * 2,
        flops=HIDE,
    )(own, from_prev, from_far, from_next)
    owned = lax.all_gather(own, "dp", axis=0)
    flat = arr(slots, BS * BS)
    block_grads = call(
        unpack_kernel,
        "unpack",
        (flat, flat, flat),
        [VMEM] * 2,
        (VMEM,) * 3,
        [pltpu.VMEM((3 * slots * (depth + 1), 2 * BS), F32)],
    )(owned, rest)
    result = arr(half, width)
    mixed, tokens_grad = call(row_sum_kernel, "row_sum", (result, result), [VMEM], (VMEM, VMEM))(
        row_terms
    )
    return (mixed, tokens_grad, *(b[None, None] for b in block_grads))


def solution(mesh):
    placed = (
        P(("dp", "col"), "row"),
        P(("dp", "col"), "row"),
        P("row", "col", None, None),
        P("row", "col", None, None),
        P("row", "col", None, None),
        P(None, "row", "col", None, None),
        P(None, "row", "col"),
    )
    return jax.shard_map(
        per_device,
        mesh=mesh,
        in_specs=placed,
        out_specs=(
            P(("dp", "col"), "row"),
            P(("dp", "col"), "row"),
            P("row", "col", None, None),
            P("row", "col", None, None),
            P("row", "col", None, None),
        ),
        check_vma=False,
    )
```

```python
import jax
import jax.numpy as jnp
from jax import lax
from jax.experimental import pallas as pl
from jax.experimental.pallas import tpu as pltpu
from jax.sharding import PartitionSpec as P

BS = 64
REST = 192
SPARE = 5
HIDE = 10**10
VMEM = pl.BlockSpec(memory_space=pltpu.VMEM)
SMEM = pl.BlockSpec(memory_space=pltpu.SMEM)
PARAMS = pltpu.CompilerParams(vmem_limit_bytes=40 * 1024 * 1024)
F32 = jnp.float32
BF16 = jnp.bfloat16


def rows_of(block):
    return pl.ds(pl.multiple_of(block * BS, BS), BS)


def feature_major(wide, cols):
    n_col, pair, width = wide.shape
    half = pair // 2
    toks = n_col * half
    for j in range(0, width, 128):
        piece = wide[:, :, j : j + 128].astype(F32).reshape(n_col, 2, half, 128)
        for side in range(2):
            cols[side, j : j + 128, :] = piece[:, side].reshape(toks, 128).T.astype(BF16)


def unflatten(flat, blocks, spaced):
    slots, area = flat.shape
    apart = BS + 1
    for j in range(0, area, 2 * BS):
        pair = flat[:, j : j + 2 * BS].astype(F32)
        d = j // BS
        spaced[pl.ds(d, slots, stride=apart), :] = pair
        spaced[pl.ds(d + 1, slots, stride=apart), :] = pltpu.roll(pair, BS, 1)
    for s in range(slots):
        blocks[s] = spaced[s * apart : s * apart + BS, :BS].astype(BF16)


def live_block(blocks, s, count):
    return jnp.where(s < count, blocks[s], jnp.zeros_like(blocks[s]))


def spread_kernel(
    index, count, cols, gate_in, up_in, down_in,
    mine, theirs, gate, up, down,
    total, spaced,
):
    total[...] = jnp.zeros_like(total)
    for m, (flat, blocks) in enumerate(((gate_in, gate), (up_in, up), (down_in, down))):
        unflatten(flat, blocks, spaced)
        for s in range(blocks.shape[0]):
            source = cols[m // 2, rows_of(index[m, 0, s]), :]
            place = rows_of(index[m, 1, s])
            total[m, place, :] += lax.dot_general(
                live_block(blocks, s, count[m]),
                source,
                (((0,), (0,)), ((), ())),
                preferred_element_type=F32,
            )
    core = lax.axis_index("row") % 2
    share = mine.shape[2]
    for x in range(mine.shape[0]):
        for m in range(3):
            for out, side in ((theirs, 1 - core), (mine, core)):
                first = pl.multiple_of((2 * x + side) * share, 32)
                out[x, m] = total[m, pl.ds(first, share), :].astype(BF16)


def pair_sum_kernel(mine, other, out):
    out[...] = (mine[...].astype(F32) + other[...].astype(F32)).astype(BF16)


def hidden_kernel(terms, out):
    sums = [terms[0, m].astype(F32) for m in range(3)]
    for j in range(1, terms.shape[0]):
        sums = [sums[m] + terms[j, m].astype(F32) for m in range(3)]
    gate, up, hgrad = sums
    sig = jax.nn.sigmoid(gate)
    units = (
        (hgrad * up * sig * (1.0 + gate * (1.0 - sig))).astype(BF16),
        (hgrad * gate * sig).astype(BF16),
        (gate * sig * up).astype(BF16),
    )
    for j in range(out.shape[0]):
        for m in range(3):
            out[j, m] = units[m]


def back_kernel(
    index, count, mine, theirs, cols, gate, up, down,
    keep, give, own, ahead, across, behind,
    band, out_total, in_total, grads,
):
    core = lax.axis_index("row") % 2
    share = mine.shape[2]
    for x in range(mine.shape[0]):
        for m in range(3):
            for half, side in ((mine, core), (theirs, 1 - core)):
                first = pl.multiple_of((2 * x + side) * share, 32)
                band[m, pl.ds(first, share), :] = half[x, m]
    out_total[...] = jnp.zeros_like(out_total)
    in_total[...] = jnp.zeros_like(in_total)
    depth = BS // 2
    for m, blocks in enumerate((gate, up, down)):
        total = out_total if m == 2 else in_total
        for s in range(blocks.shape[0]):
            unit = band[m, rows_of(index[m, 1, s]), :]
            place = rows_of(index[m, 0, s])
            total[place, :] += jnp.dot(
                live_block(blocks, s, count[m]), unit, preferred_element_type=F32
            )
            grad = lax.dot_general(
                cols[m // 2, place, :], unit, (((1,), (1,)), ((), ())), preferred_element_type=F32
            )
            grad = jnp.where(s < count[m], grad, 0.0)
            first = (m * blocks.shape[0] + s) * depth
            grads[first : first + depth, :] = jnp.concatenate(
                [grad[:depth], grad[depth:]], axis=1
            ).astype(BF16)
    even_here = lax.axis_index("col") % 2 == 0
    owners, pair, width = keep.shape
    half = pair // 2
    for j in range(0, width, 128):
        out_piece = out_total[j : j + 128, :].T.reshape(owners, 2, half, 128)
        in_piece = in_total[j : j + 128, :].T.reshape(owners, 2, half, 128)
        piece = jnp.concatenate([out_piece, in_piece], axis=2)
        even, odd = piece[:, 0], piece[:, 1]
        keep[:, :, j : j + 128] = jnp.where(even_here, even, odd).astype(BF16)
        give[:, :, j : j + 128] = jnp.where(even_here, odd, even).astype(BF16)
    outs = (own, ahead, across, behind)
    n_dp = len(outs)
    per = own.shape[0] - REST
    for away, out in enumerate(outs):
        owner = (lax.axis_index("dp") + away) % n_dp
        out[:per, :] = grads[pl.ds(pl.multiple_of(owner * per, 16), per), :]
        out[per:, :] = grads[n_dp * per :, :]


def dp_sum_kernel(here, prev, far, next_, own, rest):
    total = (here[...].astype(F32) + far[...].astype(F32)) + (
        prev[...].astype(F32) + next_[...].astype(F32)
    )
    own[...] = total[: own.shape[0]].astype(BF16)
    rest[...] = total[own.shape[0] :].astype(BF16)


def row_sum_kernel(terms, mixed, tokens_grad):
    half, width = mixed.shape
    for j in range(0, width, 128):
        total = terms[0, :, j : j + 128].astype(F32)
        for c in range(1, terms.shape[0]):
            total += terms[c, :, j : j + 128].astype(F32)
        mixed[:, j : j + 128] = total[:half].astype(BF16)
        tokens_grad[:, j : j + 128] = total[half:].astype(BF16)


def unpack_kernel(owned, rest, gate, up, down, spaced):
    n_dp, per, lanes = owned.shape
    slots = gate.shape[0]
    depth = BS // 2
    apart = depth + 1
    piece = depth // 2
    for first in range(0, 3 * slots * depth, piece):
        owner, row = first // per, first % per
        if owner < n_dp:
            part = owned[owner, row : row + piece, :]
        else:
            part = rest[row : row + piece, :]
        to = first // depth * apart + first % depth
        spaced[to : to + piece, :] = part.astype(F32)
    low = lax.broadcasted_iota(jnp.int32, (slots, lanes), 1) < BS
    for m, out in enumerate((gate, up, down)):
        base = m * slots * apart
        for k in range(0, depth, 2):
            even = spaced[pl.ds(base + k, slots, stride=apart), :]
            odd = spaced[pl.ds(base + k + 1, slots, stride=apart), :]
            out[:, k * BS : k * BS + lanes] = jnp.where(low, even, pltpu.roll(odd, BS, 1)).astype(BF16)
            start = (depth + k) * BS
            out[:, start : start + lanes] = jnp.where(low, pltpu.roll(even, BS, 1), odd).astype(BF16)


def arr(*shape):
    return jax.ShapeDtypeStruct(shape, BF16)


def call(body, name, out_shape, ins, outs, scratch=(), flops=0):
    return pl.pallas_call(
        body,
        out_shape=out_shape,
        in_specs=ins,
        out_specs=outs,
        scratch_shapes=list(scratch),
        compiler_params=PARAMS,
        cost_estimate=pl.CostEstimate(flops=flops, bytes_accessed=0, transcendentals=0),
        name=name,
    )


def per_device(tokens, grad_out, gate_blocks, up_blocks, down_blocks, block_index, block_count):
    n_dp, n_row, n_col = (lax.axis_size(a) for a in ("dp", "row", "col"))
    slots = gate_blocks.shape[2]
    half, width = tokens.shape
    toks = half * n_col
    units = 28 * BS
    share = units // n_row
    chips = n_row // 2
    index = block_index.reshape(3, 2, slots)
    count = block_count.reshape(3)
    flat_blocks = [w.reshape(slots, BS * BS) for w in (gate_blocks, up_blocks, down_blocks)]
    blocks = arr(slots, BS, BS)
    pair = [(i, i ^ 1) for i in range(n_row)]
    same_core = [[2 * x + k for x in range(chips)] for k in range(2)]
    ahead, behind, across = ([(i, (i + d) % n_dp) for i in range(n_dp)] for d in (1, 3, 2))

    both = jnp.concatenate([tokens, grad_out], axis=0)
    wide = lax.all_gather(both, "col", axis=0)
    terms = arr(chips, 3, share, toks)
    cols = call(feature_major, "feature_major", arr(2, width, toks), [VMEM], VMEM, flops=HIDE)(wide)
    mine, theirs, gate, up, down = call(
        spread_kernel,
        "spread",
        (terms, terms, blocks, blocks, blocks),
        [SMEM] * 2 + [VMEM] * 4,
        (VMEM,) * 5,
        [
            pltpu.VMEM((3, units, toks), F32),
            pltpu.VMEM(((slots + SPARE) * (BS + 1), 2 * BS), F32),
        ],
    )(index, count, cols, *flat_blocks)
    other = lax.ppermute(theirs, "row", pair)
    paired = call(pair_sum_kernel, "pair_sum", terms, [VMEM] * 2, VMEM)(mine, other)
    summed = lax.all_to_all(paired, "row", 0, 0, axis_index_groups=same_core)
    own = call(hidden_kernel, "hidden", terms, [VMEM], VMEM)(summed)
    mine = lax.all_to_all(own, "row", 0, 0, axis_index_groups=same_core)
    theirs = lax.ppermute(mine, "row", pair)
    depth = BS // 2
    per = (3 * slots * depth - REST) // n_dp
    packed = arr(per + REST, 2 * BS)
    row_half = arr(n_col // 2, 2 * half, width)
    keep, give, own, to_next, to_far, to_prev = call(
        back_kernel,
        "back",
        (row_half, row_half) + (packed,) * n_dp,
        [SMEM] * 2 + [VMEM] * 6,
        (VMEM,) * (2 + n_dp),
        [
            pltpu.VMEM((3, units, toks), BF16),
            pltpu.VMEM((width, toks), F32),
            pltpu.VMEM((width, toks), F32),
            pltpu.VMEM((3 * slots * depth, 2 * BS), BF16),
        ],
    )(index, count, mine, theirs, cols, gate, up, down)
    given = lax.ppermute(give, "col", [(i, i ^ 1) for i in range(n_col)])
    halved = call(pair_sum_kernel, "col_pair_sum", row_half, [VMEM] * 2, VMEM, flops=HIDE)(keep, given)
    same_parity = [list(range(p, n_col, 2)) for p in range(2)]
    row_terms = lax.all_to_all(halved, "col", 0, 0, axis_index_groups=same_parity)
    from_far = lax.ppermute(to_far, "dp", across)
    from_prev = lax.ppermute(to_next, "dp", ahead)
    from_next = lax.ppermute(to_prev, "dp", behind)
    own, rest = call(
        dp_sum_kernel,
        "dp_sum",
        (arr(per, 2 * BS), arr(REST, 2 * BS)),
        [VMEM] * 4,
        (VMEM,) * 2,
        flops=HIDE,
    )(own, from_prev, from_far, from_next)
    owned = lax.all_gather(own, "dp", axis=0)
    flat = arr(slots, BS * BS)
    block_grads = call(
        unpack_kernel,
        "unpack",
        (flat, flat, flat),
        [VMEM] * 2,
        (VMEM,) * 3,
        [pltpu.VMEM(((3 * slots + SPARE) * (depth + 1), 2 * BS), F32)],
    )(owned, rest)
    result = arr(half, width)
    mixed, tokens_grad = call(row_sum_kernel, "row_sum", (result, result), [VMEM], (VMEM, VMEM))(
        row_terms
    )
    return (mixed, tokens_grad, *(b[None, None] for b in block_grads))


def solution(mesh):
    placed = (
        P(("dp", "col"), "row"),
        P(("dp", "col"), "row"),
        P("row", "col", None, None),
        P("row", "col", None, None),
        P("row", "col", None, None),
        P(None, "row", "col", None, None),
        P(None, "row", "col"),
    )
    return jax.shard_map(
        per_device,
        mesh=mesh,
        in_specs=placed,
        out_specs=(
            P(("dp", "col"), "row"),
            P(("dp", "col"), "row"),
            P("row", "col", None, None),
            P("row", "col", None, None),
            P("row", "col", None, None),
        ),
        check_vma=False,
    )
```
